32 devices in a mesh: section: 4 (over y, core), tp: 4 (over z), rep: 2 (over x).
Axes of the slice: x: 2, y: 2, z: 4, core: 2. Of those that a mesh axis runs over, the one named last changes fastest.
Arguments:
- student_noise: float32 [2, 768, 64], P('rep', 'section'), may hold values from -10 to 10
- renoise_noise: float32 [2, 768, 64], P('rep', 'section'), may hold values from -10 to 10
- patch_slot: int32 [2, 768], P('rep', 'section'), may hold values from 0 to 767, each once within a row
- renoise_step: int32 [2], P('rep'), may hold values from 20 to 979
- prompt_ids: int32 [2, 256], P('rep'), may hold values from 0 to 31999
- text_table: bfloat16 [32000, 2432], P(('section', 'tp')), may hold values from -48 to 48
- student_in: bfloat16 [64, 2432], replicated, may hold values from -0.75 to 0.75
- student_qkv: bfloat16 [2432, 3, 2048], P('section', None, 'tp'), may hold values from -2 to 2
- student_out: bfloat16 [2432, 2048], P('section', 'tp'), may hold values from -0.375 to 0.375
- student_final: bfloat16 [2432, 64], replicated, may hold values from -0.125 to 0.125
- real_in: bfloat16 [64, 2432], replicated, may hold values from -0.75 to 0.75
- real_qkv: bfloat16 [2432, 3, 2048], P('section', None, 'tp'), may hold values from -2 to 2
- real_out: bfloat16 [2432, 2048], P('section', 'tp'), may hold values from -0.375 to 0.375
- real_final: bfloat16 [2432, 64], replicated, may hold values from -0.125 to 0.125
- fake_in: bfloat16 [64, 2432], replicated, may hold values from -0.75 to 0.75
- fake_qkv: bfloat16 [2432, 3, 2048], P('section', None, 'tp'), may hold values from -2 to 2
- fake_out: bfloat16 [2432, 2048], P('section', 'tp'), may hold values from -0.375 to 0.375
- fake_final: bfloat16 [2432, 64], replicated, may hold values from -0.125 to 0.125
Outputs:
- latent_grad: float32 [2, 768, 64], P('rep', 'section')
The draws below stay inside these ranges and needn't reach their ends.
All inputs are finite; a program needn't handle non-finite values. Where the reference program divides by a largest or mean magnitude, that divisor is 1e-20 or more.
Results may differ from the reference program's by a relative error of at most 0.03.
Values may be sent and summed in bfloat16 or wider, within the bound.
A program may use at most 128 MiB of HBM per device.

```python
import math
import jax
import jax.numpy as jnp
from jax import lax

D = 2432
HEADS = 32
HD = 64
CH = 64
VOCAB = 32000
PROMPT = 256
GRID_W = 64
HW = 2048
TOKENS = 768
SAMPLES = 2
N_TP = 4


def draw_student_noise(key, part):
    key = jax.random.fold_in(key, 11)
    ladder = jnp.arange(TOKENS, dtype=jnp.float32)[None, :, None] / TOKENS
    base = jnp.clip(jax.random.normal(key, (SAMPLES, TOKENS, CH), jnp.float32), -6.0, 6.0)
    return base * 0.55 * 3.0 ** ladder


def draw_renoise_noise(key, part):
    key = jax.random.fold_in(key, 23)
    ladder = jnp.arange(TOKENS, dtype=jnp.float32)[None, :, None] / TOKENS
    base = jnp.clip(jax.random.normal(key, (SAMPLES, TOKENS, CH), jnp.float32), -6.0, 6.0)
    return base * 0.55 * 3.0 ** ladder


def head_gained(pick_key, base, top):
    order = jax.random.permutation(pick_key, HEADS)
    rank = order.astype(jnp.float32) / (HEADS - 1)
    gains = jnp.float32(top) ** rank
    columns = jnp.repeat(gains, HD)
    factor = jnp.stack([columns, columns, jnp.ones((HEADS * HD,), jnp.float32)])
    return jnp.clip(base * factor[None, :, :] * D ** (-0.5), -2.0, 2.0)


def draw_student_qkv(key, part):
    key = jax.random.fold_in(key, 31)
    base_key, pick_key = jax.random.split(key)
    base = jnp.clip(jax.random.normal(base_key, (D, 3, HEADS * HD), jnp.float32), -6.0, 6.0)
    return head_gained(pick_key, base, 2.5).astype(jnp.bfloat16)


def draw_real_qkv(key, part):
    key = jax.random.fold_in(key, 37)
    base_key, pick_key = jax.random.split(key)
    base = jnp.clip(jax.random.normal(base_key, (D, 3, HEADS * HD), jnp.float32), -6.0, 6.0)
    return head_gained(pick_key, base, 2.5).astype(jnp.bfloat16)


def draw_fake_qkv(key, part):
    key = jax.random.fold_in(key, 41)
    base_key, pick_key = jax.random.split(key)
    base = jnp.clip(jax.random.normal(base_key, (D, 3, HEADS * HD), jnp.float32), -6.0, 6.0)
    return head_gained(pick_key, base, 2.5).astype(jnp.bfloat16)


def set_ends(drawn, rng, smallest, largest):
    index_at = [jax.random.randint(jax.random.fold_in(rng, axis), (), 0, length) for axis, length in enumerate(drawn.shape)]
    main_axis = drawn.shape.index(max(drawn.shape))
    beside = index_at[:main_axis] + [(index_at[main_axis] + 1) % drawn.shape[main_axis]] + index_at[main_axis + 1:]
    return drawn.at[tuple(index_at)].set(smallest).at[tuple(beside)].set(largest)


def levels(rng, shape, cuts, smallest, top_value):
    gain, own = 1.0, jax.random.fold_in(rng, 6)
    for axis_at, blocks in cuts:
        heights = jnp.exp(jax.random.uniform(jax.random.fold_in(own, axis_at), (blocks,), jnp.float32, smallest / len(cuts), top_value / len(cuts)))
        gain = gain * jnp.repeat(heights, shape[axis_at] // blocks).reshape([-1 if axis == axis_at else 1 for axis in range(len(shape))])
    return gain


def centred(own_key, shape, deviation, limit, shards=(), kind=jnp.bfloat16):
    gain = levels(own_key, shape, shards, -0.22, 0.18) if shards else 1.0
    drawn = jax.random.normal(own_key, shape, jnp.float32) * deviation * gain
    return jnp.minimum(jnp.maximum(drawn, -limit), limit).astype(kind)


def setup_inputs(seed: int = 0) -> dict:
    seeds = jax.random.split(jax.random.key(seed), 19)
    student_noise = draw_student_noise(jax.random.fold_in(seeds[18], 71), 0)
    renoise_noise = draw_renoise_noise(jax.random.fold_in(seeds[18], 71), 0)
    patch_slot = jax.vmap(lambda own: jax.random.permutation(own, TOKENS))(jax.random.split(seeds[2], SAMPLES)).reshape((SAMPLES, TOKENS)).astype(jnp.int32)
    renoise_step = jax.random.randint(seeds[3], (SAMPLES,), 20, 980).astype(jnp.int32)
    prompt_ids = set_ends(jax.random.randint(seeds[4], (SAMPLES, PROMPT), 0, VOCAB), jax.random.fold_in(seeds[4], 1), 0, VOCAB - 1).astype(jnp.int32)
    text_table = centred(seeds[5], (VOCAB, D), 8.0, 48.0, ((0, 16),))
    student_in = centred(seeds[6], (CH, D), CH ** -0.5, 0.75)
    student_qkv = draw_student_qkv(jax.random.fold_in(seeds[18], 71), 0)
    student_out = centred(seeds[8], (D, HW), (HW // 9) ** -0.5, 0.375, ((0, 4), (1, 4)))
    student_final = centred(seeds[9], (D, CH), D ** -0.5, 0.125)
    real_in = centred(seeds[10], (CH, D), CH ** -0.5, 0.75)
    real_qkv = draw_real_qkv(jax.random.fold_in(seeds[18], 71), 0)
    real_out = centred(seeds[12], (D, HW), (HW // 9) ** -0.5, 0.375, ((0, 4), (1, 4)))
    real_final = centred(seeds[13], (D, CH), D ** -0.5, 0.125)
    fake_in = centred(seeds[14], (CH, D), CH ** -0.5, 0.75)
    fake_qkv = draw_fake_qkv(jax.random.fold_in(seeds[18], 71), 0)
    fake_out = centred(seeds[16], (D, HW), (HW // 9) ** -0.5, 0.375, ((0, 4), (1, 4)))
    fake_final = centred(seeds[17], (D, CH), D ** -0.5, 0.125)
    return dict(student_noise=student_noise, renoise_noise=renoise_noise, patch_slot=patch_slot, renoise_step=renoise_step, prompt_ids=prompt_ids, text_table=text_table, student_in=student_in, student_qkv=student_qkv, student_out=student_out, student_final=student_final, real_in=real_in, real_qkv=real_qkv, real_out=real_out, real_final=real_final, fake_in=fake_in, fake_qkv=fake_qkv, fake_out=fake_out, fake_final=fake_final)


def time_embed(step_time):
    half_width = D // 2
    frequency = jnp.exp(-math.log(10000.0) * jnp.arange(half_width, dtype=jnp.float32) / half_width)
    angles = 1000.0 * step_time * frequency
    return jnp.concatenate([jnp.cos(angles), jnp.sin(angles)])

def place_embed(slots):
    quarter = D // 4
    frequency = jnp.exp(-math.log(10000.0) * jnp.arange(quarter, dtype=jnp.float32) / quarter)
    row_angle = (slots // GRID_W).astype(jnp.float32)[:, None] * frequency[None, :]
    col_angle = (slots % GRID_W).astype(jnp.float32)[:, None] * frequency[None, :]
    return jnp.concatenate([jnp.sin(row_angle), jnp.cos(row_angle), jnp.sin(col_angle), jnp.cos(col_angle)], axis=1)

def rms_norm(values):
    return values * lax.rsqrt(lax.optimization_barrier(jnp.mean(values * values, axis=-1, keepdims=True)) + 1e-06)

def attend_head(triple):
    query_head, key_head, value_head = triple
    scores = jnp.dot(query_head, key_head.T, preferred_element_type=jnp.float32) * HD ** (-0.5)
    row_max = lax.optimization_barrier(jnp.max(scores, axis=1, keepdims=True))
    expo = jnp.exp(scores - row_max)
    totals = lax.optimization_barrier(jnp.sum(expo, axis=1, keepdims=True))
    mixed = jnp.dot(expo.astype(jnp.bfloat16), value_head, preferred_element_type=jnp.float32) / totals
    return mixed.astype(jnp.bfloat16)

def network(latent, step_time, condition, w_in, w_qkv, w_out, w_final):
    hidden = jnp.dot(latent.astype(jnp.bfloat16), w_in, preferred_element_type=jnp.float32)
    hidden = hidden + condition + time_embed(step_time)[None, :]
    normed = rms_norm(hidden).astype(jnp.bfloat16)
    projected = jnp.einsum('td,dkc->tkc', normed.astype(jnp.float32), w_qkv.astype(jnp.float32)).astype(jnp.bfloat16)
    heads_query = projected[:, 0].reshape(TOKENS, HEADS, HD).transpose(1, 0, 2)
    heads_key = projected[:, 1].reshape(TOKENS, HEADS, HD).transpose(1, 0, 2)
    heads_value = projected[:, 2].reshape(TOKENS, HEADS, HD).transpose(1, 0, 2)
    mixed = lax.map(attend_head, (heads_query, heads_key, heads_value))
    mixed = mixed.transpose(1, 0, 2).reshape(TOKENS, HEADS * HD)
    group_width = HEADS * HD // N_TP

    def add_group(running, group_index):
        part_mixed = lax.dynamic_slice_in_dim(mixed, group_index * group_width, group_width, 1)
        part_weight = lax.dynamic_slice_in_dim(w_out, group_index * group_width, group_width, 1)
        group_term = jnp.dot(part_mixed, part_weight.T, preferred_element_type=jnp.float32).astype(jnp.bfloat16)
        group_term = lax.optimization_barrier(group_term).astype(jnp.float32)
        return (running + group_term, group_index)
    attended, unused = lax.scan(add_group, jnp.zeros((TOKENS, D), jnp.float32), jnp.arange(N_TP, dtype=jnp.int32))
    after = hidden + attended
    return jnp.dot(rms_norm(after).astype(jnp.bfloat16), w_final, preferred_element_type=jnp.float32)

def reference(student_noise, renoise_noise, patch_slot, renoise_step, prompt_ids, text_table, student_in, student_qkv, student_out, student_final, real_in, real_qkv, real_out, real_final, fake_in, fake_qkv, fake_out, fake_final):
    results = []
    for sample in range(SAMPLES):
        pooled = lax.optimization_barrier(jnp.mean(text_table[prompt_ids[sample]].astype(jnp.float32), axis=0))
        condition = place_embed(patch_slot[sample]) + pooled[None, :]
        start_noise = student_noise[sample]
        velocity = network(start_noise, jnp.float32(1.0), condition, student_in, student_qkv, student_out, student_final)
        clean = start_noise - velocity
        step_time = renoise_step[sample].astype(jnp.float32) / 1000.0
        noisy = (1.0 - step_time) * clean + step_time * renoise_noise[sample]
        real_velocity = network(noisy, step_time, condition, real_in, real_qkv, real_out, real_final)
        fake_velocity = network(noisy, step_time, condition, fake_in, fake_qkv, fake_out, fake_final)
        pred_real = noisy - step_time * real_velocity
        pred_fake = noisy - step_time * fake_velocity
        spread = jnp.mean(jnp.abs(clean - pred_real)) + 1e-05
        results.append((pred_fake - pred_real) / spread)
    return jnp.stack(results)
```

```python
import math

import jax
import jax.numpy as jnp
from jax import lax
from jax.experimental import pallas as pl
from jax.experimental.pallas import tpu as pltpu
from jax.sharding import PartitionSpec as P

D = 2432
HD = 64
GRID_W = 64


def time_embed(step_time):
    half_width = D // 2
    frequency = jnp.exp(-math.log(10000.0) * jnp.arange(half_width, dtype=jnp.float32) / half_width)
    angles = 1000.0 * step_time * frequency
    return jnp.concatenate([jnp.cos(angles), jnp.sin(angles)])


def place_embed(slots):
    quarter = D // 4
    frequency = jnp.exp(-math.log(10000.0) * jnp.arange(quarter, dtype=jnp.float32) / quarter)
    row_angle = (slots // GRID_W).astype(jnp.float32)[:, None] * frequency[None, :]
    col_angle = (slots % GRID_W).astype(jnp.float32)[:, None] * frequency[None, :]
    return jnp.concatenate(
        [jnp.sin(row_angle), jnp.cos(row_angle), jnp.sin(col_angle), jnp.cos(col_angle)], axis=1
    )


def rms_norm(values):
    return values * lax.rsqrt(jnp.mean(values * values, axis=-1, keepdims=True) + 1e-06)


def final_layer(after, w_final):
    return jnp.einsum(
        "ntd,ndc->ntc",
        rms_norm(after).astype(jnp.bfloat16),
        w_final,
        preferred_element_type=jnp.float32,
    )


def networks(latents, step_times, condition, w_in, w_qkv, w_out, w_final):
    count = latents.shape[0]
    tok_local = latents.shape[1]
    head_cols = w_out.shape[2]
    local_heads = head_cols // HD
    hidden = jnp.einsum(
        "ntc,ncd->ntd", latents.astype(jnp.bfloat16), w_in, preferred_element_type=jnp.float32
    )
    hidden = hidden + condition[None, :, :] + jax.vmap(time_embed)(step_times)[:, None, :]
    normed = rms_norm(hidden).astype(jnp.bfloat16)
    projected = jnp.einsum(
        "ntd,dnkc->ntkc",
        normed,
        lax.all_gather(w_qkv, "section", axis=0, tiled=True),
        preferred_element_type=jnp.float32,
    )
    projected = projected.astype(jnp.bfloat16)
    queries = projected[:, :, 0].reshape(count, tok_local, local_heads, HD)
    keys_local = projected[:, :, 1]
    values_local = projected[:, :, 2]
    row_max = jnp.full((count, local_heads, tok_local), -1e30, jnp.float32)
    key_block = lax.all_gather(keys_local, "section", axis=1, tiled=True)
    value_block = lax.all_gather(values_local, "section", axis=1, tiled=True)
    key_count = key_block.shape[1]
    key_heads = key_block.reshape(count, key_count, local_heads, HD)
    value_heads = value_block.reshape(count, key_count, local_heads, HD)
    scores = jnp.einsum(
        "nqhd,nkhd->nhqk", queries, key_heads, preferred_element_type=jnp.float32
    ) * HD ** (-0.5)
    new_max = jnp.maximum(row_max, jnp.max(scores, axis=3))
    expo = jnp.exp(scores - new_max[..., None])
    totals = jnp.sum(expo, axis=3)
    running = jnp.einsum(
        "nhqk,nkhd->nhqd",
        expo.astype(jnp.bfloat16),
        value_heads,
        preferred_element_type=jnp.float32,
    )
    row_max, totals, running = (new_max, totals, running)
    mixed = (running / totals[..., None]).astype(jnp.bfloat16)
    mixed = mixed.transpose(0, 2, 1, 3).reshape(count, tok_local, head_cols)
    group_terms = jnp.einsum(
        "ntc,rnc->ntr",
        mixed,
        lax.all_gather(w_out, "section", axis=0, tiled=True),
        preferred_element_type=jnp.float32,
    )
    attended = lax.psum(group_terms.astype(jnp.bfloat16), "tp").astype(jnp.float32)
    return final_layer(hidden + attended, w_final)


def per_device(
    student_noise,
    renoise_noise,
    patch_slot,
    renoise_step,
    prompt_ids,
    text_table,
    student_in,
    student_qkv,
    student_out,
    student_final,
    real_in,
    real_qkv,
    real_out,
    real_final,
    fake_in,
    fake_qkv,
    fake_out,
    fake_final,
):
    vocab_local = text_table.shape[0]
    first_row = lax.axis_index(("section", "tp")) * vocab_local
    prompt_row = prompt_ids[0] - first_row
    matches = (prompt_row[:, None] == jnp.arange(vocab_local, dtype=jnp.int32)[None, :]).astype(
        jnp.bfloat16
    )
    counts = jnp.sum(matches.astype(jnp.float32), axis=0).astype(jnp.bfloat16)
    partial_pool = jnp.dot(counts, text_table, preferred_element_type=jnp.float32)
    pooled = lax.psum(partial_pool, ("section", "tp")) / prompt_ids.shape[1]
    condition = place_embed(patch_slot[0]) + pooled[None, :]
    start_noise = student_noise[0]
    velocity = networks(
        start_noise[None],
        jnp.ones((1,), jnp.float32),
        condition,
        student_in[None],
        student_qkv[:, None],
        student_out[:, None],
        student_final[None],
    )[0]
    clean = start_noise - velocity
    step_time = renoise_step[0].astype(jnp.float32) / 1000.0
    noisy = (1.0 - step_time) * clean + step_time * renoise_noise[0]
    step_row = jnp.full((1,), step_time, jnp.float32)
    real_velocity = networks(
        noisy[None],
        step_row,
        condition,
        real_in[None],
        real_qkv[:, None],
        real_out[:, None],
        real_final[None],
    )[0]
    fake_velocity = networks(
        noisy[None],
        step_row,
        condition,
        fake_in[None],
        fake_qkv[:, None],
        fake_out[:, None],
        fake_final[None],
    )[0]
    pred_real = noisy - step_time * real_velocity
    pred_fake = noisy - step_time * fake_velocity
    local_spread = jnp.sum(jnp.abs(clean - pred_real))
    entries = noisy.shape[0] * lax.axis_size("section") * noisy.shape[1]
    spread = lax.psum(local_spread, "section") / entries + 1e-05
    return ((pred_fake - pred_real) / spread)[None]


MESH = pl.DeviceIdType.MESH
NETS = 3


def dot(a, b):
    return jnp.dot(a, b, preferred_element_type=jnp.float32)


def step_kernel(
    pool_ref, pack_ref, noise_ref, table_ref, time_ref, when_ref, win_ref, fin_ref,
    wq0_ref, wq1_ref, wq2_ref, wo0_ref, wo1_ref, wo2_ref,
    out_ref,
    pool_sum, pool_sec, pool_tp, pack_all, noise_all, row_hot, col_hot, zin, cond, hid, normed,
    far_send, far_recv, cross_send, cross_recv, near_send, near_recv, own, qkv,
    mix, z_send, z_recv, z_own, f_mine, f_sib, f_pair, f_cross, f_pack, flow, clean, noisy,
    send_sem, recv_sem,
):
    wq = (wq0_ref, wq1_ref, wq2_ref)
    wo = (wo0_ref, wo1_ref, wo2_ref)
    sec = lax.axis_index("section")
    tp = lax.axis_index("tp")
    core = lax.rem(sec, 2)
    sib = sec + 1 - 2 * core
    cross = lax.rem(sec + 2, 4)
    diag = lax.rem(sib + 2, 4)
    tok = pack_ref.shape[0]
    total = 4 * tok
    feat = hid.shape[2]
    half = total // 2
    chunks = ((0, half), (half, half))
    tile = tok
    counter = [0]
    sends = []

    def send(src, dst, where):
        at = counter[0]
        counter[0] += 1
        copy = pltpu.make_async_remote_copy(
            src_ref=src, dst_ref=dst, send_sem=send_sem.at[at], recv_sem=recv_sem.at[at],
            device_id=where, device_id_type=MESH,
        )
        copy.start()
        sends.append(copy)
        return copy

    def at_sec(index):
        return {"section": index}

    def at_tp(index):
        return {"tp": index}

    tps = [lax.rem(tp + step, 4) for step in range(1, 4)]
    barrier = pltpu.get_barrier_semaphore()
    for where in [at_sec(sib), at_sec(cross), at_sec(diag)] + [at_tp(index) for index in tps]:
        pl.semaphore_signal(barrier, inc=1, device_id=where, device_id_type=MESH)
    pl.semaphore_wait(barrier, 6)

    others = (sib, cross, diag)
    got_pack = [send(pack_ref, pack_all.at[sec], at_sec(index)) for index in others]
    got_pool = [send(pool_ref, pool_sec.at[slot], at_sec(index)) for slot, index in enumerate(others)]
    pack_all[sec] = pack_ref[...]
    noise_all[sec] = noise_ref[...]
    for copy in got_pool:
        copy.wait_recv()
    pool_sum[...] = (pool_ref[...] + pool_sec[0]) + (pool_sec[1] + pool_sec[2])
    got_pool = [send(pool_sum, pool_tp.at[slot], at_tp(index)) for slot, index in enumerate(tps)]
    for copy in got_pack:
        copy.wait_recv()
    for block in range(4):
        rows = pl.ds(block * tok, tok)
        packed = pack_all[block]
        lane = lax.broadcasted_iota(jnp.int32, (tok, 128), 1)
        lane = jnp.where(lane >= 64, lane - 64, lane).astype(jnp.float32)
        wide = packed.astype(jnp.float32)
        row_hot[rows, :] = jnp.where(lane == wide[:, 64:65], 1.0, 0.0).astype(jnp.bfloat16)
        col_hot[rows, :] = jnp.where(lane == wide[:, 65:66], 1.0, 0.0).astype(jnp.bfloat16)
        zin[rows, :] = packed[:, :64]
    for copy in got_pool:
        copy.wait_recv()
    pooled = (pool_sum[...] + pool_tp[0]) + (pool_tp[1] + pool_tp[2])
    pool_sum_all = pool_sec.at[0]
    pool_sum_all[...] = pooled

    def tiles(start, size, body):
        @pl.loop(0, size // tile)
        def _(index):
            body(pl.ds(pl.multiple_of(start + index * tile, tile), tile))

    def place(rows):
        for part in range(4):
            hot = row_hot if part < 2 else col_hot
            cond[part, rows, :] = dot(hot[rows, :], table_ref[part % 2]) + pool_sum_all[part : part + 1, :]

    tiles(0, total, place)

    def embed(net):
        when = 0 if net == 0 else 1

        def body(rows):
            latent = zin[rows, :]
            squares = jnp.zeros((tile, 1), jnp.float32)
            for part in range(4):
                values = dot(latent, win_ref[net, part]) + cond[part, rows, :] + time_ref[when, part]
                squares += jnp.sum(values * values, axis=1, keepdims=True)
            values = dot(latent, win_ref[net, sec]) + cond[sec, rows, :] + time_ref[when, sec]
            hid[net, rows, :] = values
            scale = lax.rsqrt(squares / (4 * feat) + 1e-06)
            normed[net, rows, :] = (values * scale).astype(jnp.bfloat16)

        tiles(0, total, body)

    def project(net):
        far = []
        for start, size in chunks:
            def body(rows):
                far_send[net, rows, :] = dot(normed[net, rows, :], wq[net][diag]).astype(jnp.bfloat16)

            tiles(start, size, body)
            rows = pl.ds(start, size)
            far.append(send(far_send.at[net, rows], far_recv.at[net, rows], at_sec(sib)))
        crossed, near = [], []
        for index, (start, size) in enumerate(chunks):
            far[index].wait_recv()

            def body(rows):
                value = dot(normed[net, rows, :], wq[net][cross])
                cross_send[net, rows, :] = (value + far_recv[net, rows, :].astype(jnp.float32)).astype(jnp.bfloat16)

            tiles(start, size, body)
            rows = pl.ds(start, size)
            crossed.append(send(cross_send.at[net, rows], cross_recv.at[net, rows], at_sec(cross)))
        for start, size in chunks:
            def body(rows):
                near_send[net, rows, :] = dot(normed[net, rows, :], wq[net][sib]).astype(jnp.bfloat16)

            tiles(start, size, body)
            rows = pl.ds(start, size)
            near.append(send(near_send.at[net, rows], near_recv.at[net, rows], at_sec(sib)))

        def body(rows):
            own[net, rows, :] = dot(normed[net, rows, :], wq[net][sec])

        tiles(0, total, body)
        return crossed, near

    def attend(net, pending):
        crossed, near = pending
        for index, (start, size) in enumerate(chunks):
            near[index].wait_recv()
            crossed[index].wait_recv()

            def body(rows):
                value = own[net, rows, :] + near_recv[net, rows, :].astype(jnp.float32)
                value = value + cross_recv[net, rows, :].astype(jnp.float32)
                qkv[net, rows, :] = value.astype(jnp.bfloat16)

            tiles(start, size, body)
        direct = []
        for start, size in chunks:
            def body(rows):
                query = qkv[net, rows, 0:128]
                keys = qkv[net, :, 128:256]
                values = qkv[net, :, 256:384]
                low = lax.broadcasted_iota(jnp.int32, (tile, 128), 1) < HD
                results = []
                for head in range(2):
                    kept = jnp.where(low if head == 0 else jnp.logical_not(low), query.astype(jnp.float32), 0.0)
                    scores = lax.dot_general(
                        kept.astype(jnp.bfloat16), keys, (((1,), (1,)), ((), ())),
                        preferred_element_type=jnp.float32,
                    ) * HD ** (-0.5)
                    expo = jnp.exp(scores - jnp.max(scores, axis=1, keepdims=True))
                    sums = jnp.sum(expo, axis=1, keepdims=True)
                    results.append(dot(expo.astype(jnp.bfloat16), values) / sums)
                mix[net, sec, rows, :] = jnp.where(low, results[0], results[1]).astype(jnp.bfloat16)

            tiles(start, size, body)
            rows = pl.ds(start, size)
            piece = mix.at[net, sec, rows]
            direct.append((send(piece, piece, at_sec(cross)), send(piece, piece, at_sec(sib))))
        return direct

    def forward(net, direct):
        result = []
        for index, (start, size) in enumerate(chunks):
            direct[index][0].wait_recv()
            piece = mix.at[net, cross, pl.ds(start, size)]
            result.append(send(piece, piece, at_sec(sib)))
        return result

    def outward(net, direct, passed):
        for index in range(len(chunks)):
            direct[index][1].wait_recv()
            passed[index].wait_recv()

        def term(slot):
            rows = pl.ds(pl.multiple_of(slot * tok, tok), tok)
            left = jnp.concatenate([mix[net, index, rows, :] for index in range(4)], axis=1)
            return lax.dot_general(
                left, wo[net][...], (((1,), (1,)), ((), ())), preferred_element_type=jnp.float32
            ).astype(jnp.bfloat16)

        pending = []
        for step in (2, 1, 3):
            z_send[net, step - 1] = term(tps[step - 1])
            pending.append(send(z_send.at[net, step - 1], z_recv.at[net, step - 1], at_tp(tps[step - 1])))
        z_own[net] = term(tp)
        return pending

    def finish(net, pending):
        for copy in pending:
            copy.wait_recv()
        rows = pl.ds(pl.multiple_of(tp * tok, tok), tok)
        summed = z_own[net].astype(jnp.float32)
        for step in range(3):
            summed = summed + z_recv[net, step].astype(jnp.float32)
        after = hid[net, rows, :] + summed
        squares = jnp.sum(after * after, axis=1, keepdims=True)
        f_mine[net, :, 0:64] = dot(after.astype(jnp.bfloat16), fin_ref[net, sec])
        f_mine[net, :, 64:128] = jnp.broadcast_to(squares, (tok, 64))
        return send(f_mine.at[net], f_sib.at[net], at_sec(sib))

    def pair(net, copy):
        copy.wait_recv()
        f_pair[net] = f_mine[net] + f_sib[net]
        return send(f_pair.at[net], f_cross.at[net], at_sec(cross))

    def scaled(net, copy):
        copy.wait_recv()
        summed = f_pair[net] + f_cross[net]
        value = summed[:, 0:64] * lax.rsqrt(summed[:, 64:128] / (4 * feat) + 1e-06)
        f_pack[net, tp, :, 0:64] = value[: tok // 2]
        f_pack[net, tp, :, 64:128] = value[tok // 2 :]
        piece = f_pack.at[net, tp]
        return [send(piece, piece, at_tp(index)) for index in tps]

    def collect(net, pending):
        for copy in pending:
            copy.wait_recv()
        for block in range(4):
            packed = f_pack[net, block]
            flow[net, pl.ds(block * tok, tok // 2), :] = packed[:, 0:64]
            flow[net, pl.ds(block * tok + tok // 2, tok // 2), :] = packed[:, 64:128]

    embed(0)
    pending = project(0)
    got_noise = [send(noise_ref, noise_all.at[sec], at_sec(index)) for index in others]
    direct = attend(0, pending)
    passed = forward(0, direct)
    pending = outward(0, direct, passed)
    collect(0, scaled(0, pair(0, finish(0, pending))))
    for copy in got_noise:
        copy.wait_recv()
    moment = when_ref[0:1, 0:64]
    for block in range(4):
        rows = pl.ds(block * tok, tok)
        both = noise_all[block]
        start = both[:, 0:64] - flow[0, rows, :]
        clean[rows, :] = start
        mixed = (1.0 - moment) * start + moment * both[:, 64:128]
        noisy[rows, :] = mixed
        zin[rows, :] = mixed.astype(jnp.bfloat16)
    pending = {}
    for net in (1, 2):
        embed(net)
        pending[net] = project(net)
    direct = {net: attend(net, pending[net]) for net in (1, 2)}
    passed = {net: forward(net, direct[net]) for net in (1, 2)}
    pending = {net: outward(net, direct[net], passed[net]) for net in (1, 2)}
    pending = {net: finish(net, pending[net]) for net in (1, 2)}
    pending = {net: pair(net, pending[net]) for net in (1, 2)}
    pending = {net: scaled(net, pending[net]) for net in (1, 2)}
    for net in (1, 2):
        collect(net, pending[net])
    real = noisy[...] - moment * flow[1]
    spread = jnp.sum(jnp.abs(clean[...] - real), axis=1, keepdims=True)
    spread = jnp.sum(spread, axis=0, keepdims=True) / (total * 64) + 1e-05
    rows = pl.ds(pl.multiple_of(sec * tok, tok), tok)
    real = noisy[rows, :] - moment * flow[1, rows, :]
    fake = noisy[rows, :] - moment * flow[2, rows, :]
    out_ref[...] = (fake - real) / spread
    for copy in sends:
        copy.wait_send()


def step_call(*operands):
    tok, feat, total = operands[1].shape[0], operands[0].shape[1], 4 * operands[1].shape[0]
    f32, bf16 = jnp.float32, jnp.bfloat16
    shapes = [
        ((8, feat), f32), ((3, 8, feat), f32), ((3, 8, feat), f32),
        ((4, tok, 128), bf16), ((4, tok, 128), f32),
        ((total, 128), bf16), ((total, 128), bf16), ((total, 64), bf16),
        ((4, total, feat), f32), ((NETS, total, feat), f32), ((NETS, total, feat), bf16),
    ]
    shapes += [((NETS, total, 384), bf16)] * 6
    shapes += [((NETS, total, 384), f32), ((NETS, total, 384), bf16)]
    shapes += [((NETS, 4, total, 128), bf16), ((NETS, 3, tok, feat), bf16), ((NETS, 3, tok, feat), bf16)]
    shapes += [((NETS, tok, feat), bf16)] + [((NETS, tok, 128), f32)] * 4
    shapes += [((NETS, 4, tok // 2, 128), f32), ((NETS, total, 64), f32), ((total, 64), f32), ((total, 64), f32)]
    count = 3 * 4 + NETS * (6 + 6 + 3 + 2 + 3)
    return pl.pallas_call(
        step_kernel,
        out_shape=jax.ShapeDtypeStruct((tok, 64), f32),
        in_specs=[pl.BlockSpec(memory_space=pltpu.VMEM)] * len(operands),
        out_specs=pl.BlockSpec(memory_space=pltpu.VMEM),
        scratch_shapes=[pltpu.VMEM(shape, kind) for shape, kind in shapes]
        + [pltpu.SemaphoreType.DMA((count,)), pltpu.SemaphoreType.DMA((count,))],
        compiler_params=pltpu.CompilerParams(
            collective_id=0, has_side_effects=True, vmem_limit_bytes=60 * 2**20
        ),
    )(*operands)


def by_features(
    student_noise, renoise_noise, patch_slot, renoise_step, prompt_ids, text_table,
    student_in, student_qkv, student_out, student_final,
    real_in, real_qkv, real_out, real_final,
    fake_in, fake_qkv, fake_out, fake_final,
):
    f32, bf16 = jnp.float32, jnp.bfloat16
    quarter = D // 4
    vocab_local = text_table.shape[0]
    first_row = lax.axis_index(("section", "tp")) * vocab_local
    prompt_row = prompt_ids[0] - first_row
    matches = (prompt_row[:, None] == jnp.arange(vocab_local, dtype=jnp.int32)[None, :]).astype(bf16)
    counts = jnp.sum(matches.astype(f32), axis=0).astype(bf16)
    pool = jnp.dot(counts, text_table, preferred_element_type=f32) / prompt_ids.shape[1]
    pool = jnp.pad(pool.reshape(4, quarter), ((0, 4), (0, 0)))
    slots = patch_slot[0]
    places = jnp.stack([slots // GRID_W, slots % GRID_W], axis=1).astype(bf16)
    pack = jnp.concatenate([student_noise[0].astype(bf16), jnp.pad(places, ((0, 0), (0, 62)))], axis=1)
    noise = jnp.concatenate([student_noise[0], renoise_noise[0]], axis=1)
    frequency = jnp.exp(-math.log(10000.0) * jnp.arange(quarter, dtype=f32) / quarter)
    angle = jnp.arange(64, dtype=f32)[:, None] * frequency[None, :]
    table = jnp.stack([jnp.sin(angle), jnp.cos(angle)])
    high = lax.reduce_precision(table, 8, 7)
    table = jnp.concatenate([high, table - high], axis=1).astype(bf16)
    moment = renoise_step[0].astype(f32) / 1000.0
    times = jnp.stack([time_embed(jnp.float32(1.0)), time_embed(moment)]).reshape(2, 4, 1, quarter)
    w_in = jnp.stack([student_in, real_in, fake_in]).reshape(NETS, 64, 4, quarter).transpose(0, 2, 1, 3)
    w_final = jnp.stack([student_final, real_final, fake_final]).reshape(NETS, 4, quarter, 64)

    def by_target(weight):
        return weight.reshape(quarter, 3, 4, 128).transpose(2, 0, 1, 3).reshape(4, quarter, 384)

    result = step_call(
        pool, pack, noise, table, times, jnp.full((8, 128), moment, f32), w_in, w_final,
        by_target(student_qkv), by_target(real_qkv), by_target(fake_qkv),
        student_out, real_out, fake_out,
    )
    return result[None]


def solution(mesh):
    placed = (
        P("rep", "section", None),
        P("rep", "section", None),
        P("rep", "section"),
        P("rep"),
        P("rep", None),
        P(("section", "tp"), None),
        P(),
        P("section", None, "tp"),
        P("section", "tp"),
        P(),
        P(),
        P("section", None, "tp"),
        P("section", "tp"),
        P(),
        P(),
        P("section", None, "tp"),
        P("section", "tp"),
        P(),
    )
    sizes = dict(mesh.shape)
    small = sizes["section"] == 4 and sizes["tp"] == 4 and sizes["rep"] == 2
    return jax.shard_map(
        by_features if small else per_device, mesh=mesh, in_specs=placed, out_specs=P("rep", "section", None), check_vma=False
    )
```

```python
import math

import jax
import jax.numpy as jnp
from jax import lax
from jax.experimental import pallas as pl
from jax.experimental.pallas import tpu as pltpu
from jax.sharding import PartitionSpec as P

D = 2432
HD = 64
GRID_W = 64


def time_embed(step_time):
    half_width = D // 2
    frequency = jnp.exp(-math.log(10000.0) * jnp.arange(half_width, dtype=jnp.float32) / half_width)
    angles = 1000.0 * step_time * frequency
    return jnp.concatenate([jnp.cos(angles), jnp.sin(angles)])


def place_embed(slots):
    quarter = D // 4
    frequency = jnp.exp(-math.log(10000.0) * jnp.arange(quarter, dtype=jnp.float32) / quarter)
    row_angle = (slots // GRID_W).astype(jnp.float32)[:, None] * frequency[None, :]
    col_angle = (slots % GRID_W).astype(jnp.float32)[:, None] * frequency[None, :]
    return jnp.concatenate(
        [jnp.sin(row_angle), jnp.cos(row_angle), jnp.sin(col_angle), jnp.cos(col_angle)], axis=1
    )


def rms_norm(values):
    return values * lax.rsqrt(jnp.mean(values * values, axis=-1, keepdims=True) + 1e-06)


def final_layer(after, w_final):
    return jnp.einsum(
        "ntd,ndc->ntc",
        rms_norm(after).astype(jnp.bfloat16),
        w_final,
        preferred_element_type=jnp.float32,
    )


def networks(latents, step_times, condition, w_in, w_qkv, w_out, w_final):
    count = latents.shape[0]
    tok_local = latents.shape[1]
    head_cols = w_out.shape[2]
    local_heads = head_cols // HD
    hidden = jnp.einsum(
        "ntc,ncd->ntd", latents.astype(jnp.bfloat16), w_in, preferred_element_type=jnp.float32
    )
    hidden = hidden + condition[None, :, :] + jax.vmap(time_embed)(step_times)[:, None, :]
    normed = rms_norm(hidden).astype(jnp.bfloat16)
    projected = jnp.einsum(
        "ntd,dnkc->ntkc",
        normed,
        lax.all_gather(w_qkv, "section", axis=0, tiled=True),
        preferred_element_type=jnp.float32,
    )
    projected = projected.astype(jnp.bfloat16)
    queries = projected[:, :, 0].reshape(count, tok_local, local_heads, HD)
    keys_local = projected[:, :, 1]
    values_local = projected[:, :, 2]
    row_max = jnp.full((count, local_heads, tok_local), -1e30, jnp.float32)
    key_block = lax.all_gather(keys_local, "section", axis=1, tiled=True)
    value_block = lax.all_gather(values_local, "section", axis=1, tiled=True)
    key_count = key_block.shape[1]
    key_heads = key_block.reshape(count, key_count, local_heads, HD)
    value_heads = value_block.reshape(count, key_count, local_heads, HD)
    scores = jnp.einsum(
        "nqhd,nkhd->nhqk", queries, key_heads, preferred_element_type=jnp.float32
    ) * HD ** (-0.5)
    new_max = jnp.maximum(row_max, jnp.max(scores, axis=3))
    expo = jnp.exp(scores - new_max[..., None])
    totals = jnp.sum(expo, axis=3)
    running = jnp.einsum(
        "nhqk,nkhd->nhqd",
        expo.astype(jnp.bfloat16),
        value_heads,
        preferred_element_type=jnp.float32,
    )
    row_max, totals, running = (new_max, totals, running)
    mixed = (running / totals[..., None]).astype(jnp.bfloat16)
    mixed = mixed.transpose(0, 2, 1, 3).reshape(count, tok_local, head_cols)
    group_terms = jnp.einsum(
        "ntc,rnc->ntr",
        mixed,
        lax.all_gather(w_out, "section", axis=0, tiled=True),
        preferred_element_type=jnp.float32,
    )
    attended = lax.psum(group_terms.astype(jnp.bfloat16), "tp").astype(jnp.float32)
    return final_layer(hidden + attended, w_final)


def per_device(
    student_noise,
    renoise_noise,
    patch_slot,
    renoise_step,
    prompt_ids,
    text_table,
    student_in,
    student_qkv,
    student_out,
    student_final,
    real_in,
    real_qkv,
    real_out,
    real_final,
    fake_in,
    fake_qkv,
    fake_out,
    fake_final,
):
    vocab_local = text_table.shape[0]
    first_row = lax.axis_index(("section", "tp")) * vocab_local
    prompt_row = prompt_ids[0] - first_row
    matches = (prompt_row[:, None] == jnp.arange(vocab_local, dtype=jnp.int32)[None, :]).astype(
        jnp.bfloat16
    )
    counts = jnp.sum(matches.astype(jnp.float32), axis=0).astype(jnp.bfloat16)
    partial_pool = jnp.dot(counts, text_table, preferred_element_type=jnp.float32)
    pooled = lax.psum(partial_pool, ("section", "tp")) / prompt_ids.shape[1]
    condition = place_embed(patch_slot[0]) + pooled[None, :]
    start_noise = student_noise[0]
    velocity = networks(
        start_noise[None],
        jnp.ones((1,), jnp.float32),
        condition,
        student_in[None],
        student_qkv[:, None],
        student_out[:, None],
        student_final[None],
    )[0]
    clean = start_noise - velocity
    step_time = renoise_step[0].astype(jnp.float32) / 1000.0
    noisy = (1.0 - step_time) * clean + step_time * renoise_noise[0]
    step_row = jnp.full((1,), step_time, jnp.float32)
    real_velocity = networks(
        noisy[None],
        step_row,
        condition,
        real_in[None],
        real_qkv[:, None],
        real_out[:, None],
        real_final[None],
    )[0]
    fake_velocity = networks(
        noisy[None],
        step_row,
        condition,
        fake_in[None],
        fake_qkv[:, None],
        fake_out[:, None],
        fake_final[None],
    )[0]
    pred_real = noisy - step_time * real_velocity
    pred_fake = noisy - step_time * fake_velocity
    local_spread = jnp.sum(jnp.abs(clean - pred_real))
    entries = noisy.shape[0] * lax.axis_size("section") * noisy.shape[1]
    spread = lax.psum(local_spread, "section") / entries + 1e-05
    return ((pred_fake - pred_real) / spread)[None]


MESH = pl.DeviceIdType.MESH
NETS = 3


def dot(a, b):
    return jnp.dot(a, b, preferred_element_type=jnp.float32)


def step_kernel(
    pool_ref, pack_ref, noise_ref, table_ref, time_ref, when_ref, win_ref, fin0_ref, fin1_ref, fin2_ref,
    wq0_ref, wq1_ref, wq2_ref, wo0_ref, wo1_ref, wo2_ref,
    out_ref,
    pool_sum, pool_sec, pool_tp, pack_all, noise_all, row_hot, col_hot, zin, cond, hid, normed,
    far_send, far_recv, cross_send, cross_recv, near_send, near_recv, own, qkv,
    mix, mix_send, wo_all, f_mine, f_sib, f_pair, f_cross, f_pack, flow, clean, noisy,
    send_sem, recv_sem,
):
    wq = (wq0_ref, wq1_ref, wq2_ref)
    wo = (wo0_ref, wo1_ref, wo2_ref)
    fin = (fin0_ref, fin1_ref, fin2_ref)
    rep = lax.axis_index("rep")
    peer = 1 - rep
    sec = lax.axis_index("section")
    tp = lax.axis_index("tp")
    core = lax.rem(sec, 2)
    sib = sec + 1 - 2 * core
    cross = lax.rem(sec + 2, 4)
    diag = lax.rem(sib + 2, 4)
    tok = pack_ref.shape[0]
    total = 4 * tok
    feat = hid.shape[2]
    half = total // 2
    chunks = ((0, half), (half, half))
    tile = tok
    counter = [0]
    sends = []

    def send(src, dst, where):
        at = counter[0]
        counter[0] += 1
        copy = pltpu.make_async_remote_copy(
            src_ref=src, dst_ref=dst, send_sem=send_sem.at[at], recv_sem=recv_sem.at[at],
            device_id=where, device_id_type=MESH,
        )
        copy.start()
        sends.append(copy)
        return copy

    def at_sec(index):
        return {"section": index}

    def at_tp(index):
        return {"tp": index}

    tps = [lax.rem(tp + step, 4) for step in range(1, 4)]
    barrier = pltpu.get_barrier_semaphore()
    for where in [at_sec(sib), at_sec(cross), at_sec(diag)] + [at_tp(index) for index in tps] + [{"rep": peer}]:
        pl.semaphore_signal(barrier, inc=1, device_id=where, device_id_type=MESH)
    pl.semaphore_wait(barrier, 7)

    others = (sib, cross, diag)
    got_pack = [send(pack_ref, pack_all.at[sec], at_sec(index)) for index in others]
    got_pool = [send(pool_ref, pool_sec.at[slot], at_sec(index)) for slot, index in enumerate(others)]
    part_rows = feat // 2
    mine = pl.ds(pl.multiple_of(rep * part_rows, 16), part_rows)

    def spread_weight(net):
        wo_all[net, tp] = wo[net][...]
        return [send(wo[net].at[mine], wo_all.at[net, tp, mine], at_tp(tps[step])) for step in (1, 0, 2)]

    def share_weight(net, pending):
        result = []
        for copy, step in zip(pending, (2, 1, 3)):
            copy.wait_recv()
            piece = wo_all.at[net, lax.rem(tp + 4 - step, 4), mine]
            result.append(send(piece, piece, {"rep": peer}))
        return result

    pack_all[sec] = pack_ref[...]
    noise_all[sec] = noise_ref[...]
    for copy in got_pool:
        copy.wait_recv()
    pool_sum[...] = (pool_ref[...] + pool_sec[0]) + (pool_sec[1] + pool_sec[2])
    got_pool = [send(pool_sum, pool_tp.at[slot], at_tp(index)) for slot, index in enumerate(tps)]
    halves = {0: spread_weight(0)}
    for copy in got_pack:
        copy.wait_recv()
    for block in range(4):
        rows = pl.ds(block * tok, tok)
        packed = pack_all[block]
        lane = lax.broadcasted_iota(jnp.int32, (tok, 128), 1)
        lane = jnp.where(lane >= 64, lane - 64, lane).astype(jnp.float32)
        wide = packed.astype(jnp.float32)
        row_hot[rows, :] = jnp.where(lane == wide[:, 64:65], 1.0, 0.0).astype(jnp.bfloat16)
        col_hot[rows, :] = jnp.where(lane == wide[:, 65:66], 1.0, 0.0).astype(jnp.bfloat16)
        zin[rows, :] = packed[:, :64]
    for copy in got_pool:
        copy.wait_recv()
    pooled = (pool_sum[...] + pool_tp[0]) + (pool_tp[1] + pool_tp[2])
    pool_sum_all = pool_sec.at[0]
    pool_sum_all[...] = pooled

    def tiles(start, size, body):
        @pl.loop(0, size // tile)
        def _(index):
            body(pl.ds(pl.multiple_of(start + index * tile, tile), tile))

    def place(rows):
        for part in range(4):
            hot = row_hot if part < 2 else col_hot
            cond[part, rows, :] = dot(hot[rows, :], table_ref[part % 2]) + pool_sum_all[part : part + 1, :]

    tiles(0, total, place)

    def embed(net):
        when = 0 if net == 0 else 1

        def body(rows):
            latent = zin[rows, :]
            squares = jnp.zeros((tile, 1), jnp.float32)
            for part in range(4):
                values = dot(latent, win_ref[net, part]) + cond[part, rows, :] + time_ref[when, part]
                squares += jnp.sum(values * values, axis=1, keepdims=True)
            values = dot(latent, win_ref[net, sec]) + cond[sec, rows, :] + time_ref[when, sec]
            hid[net, rows, :] = values
            scale = lax.rsqrt(squares / (4 * feat) + 1e-06)
            normed[net, rows, :] = (values * scale).astype(jnp.bfloat16)

        tiles(0, total, body)

    def part_of(net, rows, target):
        columns = pl.ds(pl.multiple_of(target * 128, 128), 128)
        left = normed[net, rows, :]
        return jnp.concatenate([dot(left, wq[net][kind, :, columns]) for kind in range(3)], axis=1)

    def project(net):
        far = []
        for start, size in chunks:
            def body(rows):
                far_send[net, rows, :] = part_of(net, rows, diag).astype(jnp.bfloat16)

            tiles(start, size, body)
            rows = pl.ds(start, size)
            far.append(send(far_send.at[net, rows], far_recv.at[net, rows], at_sec(sib)))
        crossed, near = [], []
        for index, (start, size) in enumerate(chunks):
            far[index].wait_recv()

            def body(rows):
                value = part_of(net, rows, cross)
                cross_send[net, rows, :] = (value + far_recv[net, rows, :].astype(jnp.float32)).astype(jnp.bfloat16)

            tiles(start, size, body)
            rows = pl.ds(start, size)
            crossed.append(send(cross_send.at[net, rows], cross_recv.at[net, rows], at_sec(cross)))
        for start, size in chunks:
            def body(rows):
                near_send[net, rows, :] = part_of(net, rows, sib).astype(jnp.bfloat16)

            tiles(start, size, body)
            rows = pl.ds(start, size)
            near.append(send(near_send.at[net, rows], near_recv.at[net, rows], at_sec(sib)))

        def body(rows):
            own[net, rows, :] = part_of(net, rows, sec)

        tiles(0, total, body)
        return crossed, near

    def attend(net, pending):
        crossed, near = pending
        for index, (start, size) in enumerate(chunks):
            near[index].wait_recv()
            crossed[index].wait_recv()

            def body(rows):
                value = own[net, rows, :] + near_recv[net, rows, :].astype(jnp.float32)
                value = value + cross_recv[net, rows, :].astype(jnp.float32)
                qkv[net, rows, :] = value.astype(jnp.bfloat16)

            tiles(start, size, body)
        keys = qkv[net, :, 128:256]
        values = qkv[net, :, 256:384]
        low = lax.broadcasted_iota(jnp.int32, (tok, 128), 1) < HD

        def block(index):
            rows = pl.ds(pl.multiple_of(index * tok, tok), tok)
            query = qkv[net, rows, 0:128].astype(jnp.float32)
            results = []
            for head in range(2):
                kept = jnp.where(low if head == 0 else jnp.logical_not(low), query, 0.0)
                scores = lax.dot_general(
                    kept.astype(jnp.bfloat16), keys, (((1,), (1,)), ((), ())),
                    preferred_element_type=jnp.float32,
                ) * HD ** (-0.5)
                expo = jnp.exp(scores - jnp.max(scores, axis=1, keepdims=True))
                sums = jnp.sum(expo, axis=1, keepdims=True)
                results.append(dot(expo.astype(jnp.bfloat16), values) / sums)
            return jnp.where(low, results[0], results[1]).astype(jnp.bfloat16)

        pending = []
        for step in (2, 1, 3):
            mix_send[net, step - 1] = block(tps[step - 1])
            pending.append(send(mix_send.at[net, step - 1], mix.at[net, sec, tp], at_tp(tps[step - 1])))
        mix[net, sec, tp] = block(tp)
        return pending

    def gather(net, pending):
        for copy in pending:
            copy.wait_recv()
        piece = mix.at[net, sec]
        return send(piece, piece, at_sec(cross)), send(piece, piece, at_sec(sib))

    def forward(net, direct):
        direct[0].wait_recv()
        piece = mix.at[net, cross]
        return send(piece, piece, at_sec(sib))

    def finish(net, direct, passed, shared):
        for copy in shared:
            copy.wait_recv()
        direct[1].wait_recv()
        passed.wait_recv()
        rows = pl.ds(pl.multiple_of(tp * tok, tok), tok)
        after = hid[net, rows, :]
        for group in range(4):
            left = jnp.concatenate([mix[net, index, group] for index in range(4)], axis=1)
            after = after + lax.dot_general(
                left, wo_all[net, group], (((1,), (1,)), ((), ())), preferred_element_type=jnp.float32
            )
        squares = jnp.sum(after * after, axis=1, keepdims=True)
        f_mine[net, :, 0:64] = dot(after.astype(jnp.bfloat16), fin[net][sec])
        f_mine[net, :, 64:128] = jnp.broadcast_to(squares, (tok, 64))
        return send(f_mine.at[net], f_sib.at[net], at_sec(sib))

    def pair(net, copy):
        copy.wait_recv()
        f_pair[net] = f_mine[net] + f_sib[net]
        return send(f_pair.at[net], f_cross.at[net], at_sec(cross))

    def scaled(net, copy):
        copy.wait_recv()
        summed = f_pair[net] + f_cross[net]
        value = summed[:, 0:64] * lax.rsqrt(summed[:, 64:128] / (4 * feat) + 1e-06)
        f_pack[net, tp, :, 0:64] = value[: tok // 2]
        f_pack[net, tp, :, 64:128] = value[tok // 2 :]
        piece = f_pack.at[net, tp]
        return [send(piece, piece, at_tp(index)) for index in tps]

    def collect(net, pending):
        for copy in pending:
            copy.wait_recv()
        for block in range(4):
            packed = f_pack[net, block]
            flow[net, pl.ds(block * tok, tok // 2), :] = packed[:, 0:64]
            flow[net, pl.ds(block * tok + tok // 2, tok // 2), :] = packed[:, 64:128]

    embed(0)
    pending = project(0)
    got_noise = [send(noise_ref, noise_all.at[sec], at_sec(index)) for index in others]
    moved = attend(0, pending)
    shared = {0: share_weight(0, halves[0])}
    direct = gather(0, moved)
    for net in (1, 2):
        halves[net] = spread_weight(net)
    passed = forward(0, direct)
    collect(0, scaled(0, pair(0, finish(0, direct, passed, shared[0]))))
    for copy in got_noise:
        copy.wait_recv()
    moment = when_ref[0:1, 0:64]
    for block in range(4):
        rows = pl.ds(block * tok, tok)
        both = noise_all[block]
        start = both[:, 0:64] - flow[0, rows, :]
        clean[rows, :] = start
        mixed = (1.0 - moment) * start + moment * both[:, 64:128]
        noisy[rows, :] = mixed
        zin[rows, :] = mixed.astype(jnp.bfloat16)
    pending = {}
    for net in (1, 2):
        embed(net)
        pending[net] = project(net)
    moved = {}
    for net in (1, 2):
        shared[net] = share_weight(net, halves[net])
        moved[net] = attend(net, pending[net])
    direct = {net: gather(net, moved[net]) for net in (1, 2)}
    passed = {net: forward(net, direct[net]) for net in (1, 2)}
    pending = {net: finish(net, direct[net], passed[net], shared[net]) for net in (1, 2)}
    pending = {net: pair(net, pending[net]) for net in (1, 2)}
    pending = {net: scaled(net, pending[net]) for net in (1, 2)}
    for net in (1, 2):
        collect(net, pending[net])
    real = noisy[...] - moment * flow[1]
    spread = jnp.sum(jnp.abs(clean[...] - real), axis=1, keepdims=True)
    spread = jnp.sum(spread, axis=0, keepdims=True) / (total * 64) + 1e-05
    rows = pl.ds(pl.multiple_of(sec * tok, tok), tok)
    real = noisy[rows, :] - moment * flow[1, rows, :]
    fake = noisy[rows, :] - moment * flow[2, rows, :]
    out_ref[...] = (fake - real) / spread
    for copy in sends:
        copy.wait_send()


def step_call(*operands):
    tok, feat, total = operands[1].shape[0], operands[0].shape[1], 4 * operands[1].shape[0]
    f32, bf16 = jnp.float32, jnp.bfloat16
    shapes = [
        ((8, feat), f32), ((3, 8, feat), f32), ((3, 8, feat), f32),
        ((4, tok, 128), bf16), ((4, tok, 128), f32),
        ((total, 128), bf16), ((total, 128), bf16), ((total, 64), bf16),
        ((4, total, feat), f32), ((NETS, total, feat), f32), ((NETS, total, feat), bf16),
    ]
    shapes += [((NETS, total, 384), bf16)] * 6
    shapes += [((NETS, total, 384), f32), ((NETS, total, 384), bf16)]
    shapes += [((NETS, 4, 4, tok, 128), bf16), ((NETS, 3, tok, 128), bf16), ((NETS, 4, feat, 512), bf16)]
    shapes += [((NETS, tok, 128), f32)] * 4
    shapes += [((NETS, 4, tok // 2, 128), f32), ((NETS, total, 64), f32), ((total, 64), f32), ((total, 64), f32)]
    count = 3 * 4 + NETS * (6 + 3 + 3 + 6 + 2 + 3)
    return pl.pallas_call(
        step_kernel,
        out_shape=jax.ShapeDtypeStruct((tok, 64), f32),
        in_specs=[pl.BlockSpec(memory_space=pltpu.VMEM)] * len(operands),
        out_specs=pl.BlockSpec(memory_space=pltpu.VMEM),
        scratch_shapes=[pltpu.VMEM(shape, kind) for shape, kind in shapes]
        + [pltpu.SemaphoreType.DMA((count,)), pltpu.SemaphoreType.DMA((count,))],
        compiler_params=pltpu.CompilerParams(
            collective_id=0, has_side_effects=True, vmem_limit_bytes=60 * 2**20
        ),
    )(*operands)


def by_features(
    student_noise, renoise_noise, patch_slot, renoise_step, prompt_ids, text_table,
    student_in, student_qkv, student_out, student_final,
    real_in, real_qkv, real_out, real_final,
    fake_in, fake_qkv, fake_out, fake_final,
):
    f32, bf16 = jnp.float32, jnp.bfloat16
    quarter = D // 4
    vocab_local = text_table.shape[0]
    first_row = lax.axis_index(("section", "tp")) * vocab_local
    prompt_row = prompt_ids[0] - first_row
    matches = (prompt_row[:, None] == jnp.arange(vocab_local, dtype=jnp.int32)[None, :]).astype(bf16)
    counts = jnp.sum(matches.astype(f32), axis=0).astype(bf16)
    pool = jnp.dot(counts, text_table, preferred_element_type=f32) / prompt_ids.shape[1]
    pool = jnp.pad(pool.reshape(4, quarter), ((0, 4), (0, 0)))
    slots = patch_slot[0]
    places = jnp.stack([slots // GRID_W, slots % GRID_W], axis=1).astype(bf16)
    pack = jnp.concatenate([student_noise[0].astype(bf16), jnp.pad(places, ((0, 0), (0, 62)))], axis=1)
    noise = jnp.concatenate([student_noise[0], renoise_noise[0]], axis=1)
    frequency = jnp.exp(-math.log(10000.0) * jnp.arange(quarter, dtype=f32) / quarter)
    angle = jnp.arange(64, dtype=f32)[:, None] * frequency[None, :]
    table = jnp.stack([jnp.sin(angle), jnp.cos(angle)])
    high = lax.reduce_precision(table, 8, 7)
    table = jnp.concatenate([high, table - high], axis=1).astype(bf16)
    moment = renoise_step[0].astype(f32) / 1000.0
    times = jnp.stack([time_embed(jnp.float32(1.0)), time_embed(moment)]).reshape(2, 4, 1, quarter)
    w_in = jnp.stack([student_in, real_in, fake_in]).reshape(NETS, 64, 4, quarter).transpose(0, 2, 1, 3)
    w_final = [each.reshape(4, quarter, 64) for each in (student_final, real_final, fake_final)]

    def by_kind(weight):
        return weight.transpose(1, 0, 2)

    result = step_call(
        pool, pack, noise, table, times, jnp.full((8, 128), moment, f32), w_in, *w_final,
        by_kind(student_qkv), by_kind(real_qkv), by_kind(fake_qkv),
        student_out, real_out, fake_out,
    )
    return result[None]


def solution(mesh):
    placed = (
        P("rep", "section", None),
        P("rep", "section", None),
        P("rep", "section"),
        P("rep"),
        P("rep", None),
        P(("section", "tp"), None),
        P(),
        P("section", None, "tp"),
        P("section", "tp"),
        P(),
        P(),
        P("section", None, "tp"),
        P("section", "tp"),
        P(),
        P(),
        P("section", None, "tp"),
        P("section", "tp"),
        P(),
    )
    sizes = dict(mesh.shape)
    small = sizes["section"] == 4 and sizes["tp"] == 4 and sizes["rep"] == 2
    return jax.shard_map(
        by_features if small else per_device, mesh=mesh, in_specs=placed, out_specs=P("rep", "section", None), check_vma=False
    )
```

```python
import math

import jax
import jax.numpy as jnp
from jax import lax
from jax.experimental import pallas as pl
from jax.experimental.pallas import tpu as pltpu
from jax.sharding import PartitionSpec as P

D = 2432
HD = 64
GRID_W = 64


def time_embed(step_time):
    half_width = D // 2
    frequency = jnp.exp(-math.log(10000.0) * jnp.arange(half_width, dtype=jnp.float32) / half_width)
    angles = 1000.0 * step_time * frequency
    return jnp.concatenate([jnp.cos(angles), jnp.sin(angles)])


def place_embed(slots):
    quarter = D // 4
    frequency = jnp.exp(-math.log(10000.0) * jnp.arange(quarter, dtype=jnp.float32) / quarter)
    row_angle = (slots // GRID_W).astype(jnp.float32)[:, None] * frequency[None, :]
    col_angle = (slots % GRID_W).astype(jnp.float32)[:, None] * frequency[None, :]
    return jnp.concatenate(
        [jnp.sin(row_angle), jnp.cos(row_angle), jnp.sin(col_angle), jnp.cos(col_angle)], axis=1
    )


def rms_norm(values):
    return values * lax.rsqrt(jnp.mean(values * values, axis=-1, keepdims=True) + 1e-06)


def final_layer(after, w_final):
    return jnp.einsum(
        "ntd,ndc->ntc",
        rms_norm(after).astype(jnp.bfloat16),
        w_final,
        preferred_element_type=jnp.float32,
    )


def networks(latents, step_times, condition, w_in, w_qkv, w_out, w_final):
    count = latents.shape[0]
    tok_local = latents.shape[1]
    head_cols = w_out.shape[2]
    local_heads = head_cols // HD
    hidden = jnp.einsum(
        "ntc,ncd->ntd", latents.astype(jnp.bfloat16), w_in, preferred_element_type=jnp.float32
    )
    hidden = hidden + condition[None, :, :] + jax.vmap(time_embed)(step_times)[:, None, :]
    normed = rms_norm(hidden).astype(jnp.bfloat16)
    projected = jnp.einsum(
        "ntd,dnkc->ntkc",
        normed,
        lax.all_gather(w_qkv, "section", axis=0, tiled=True),
        preferred_element_type=jnp.float32,
    )
    projected = projected.astype(jnp.bfloat16)
    queries = projected[:, :, 0].reshape(count, tok_local, local_heads, HD)
    keys_local = projected[:, :, 1]
    values_local = projected[:, :, 2]
    row_max = jnp.full((count, local_heads, tok_local), -1e30, jnp.float32)
    key_block = lax.all_gather(keys_local, "section", axis=1, tiled=True)
    value_block = lax.all_gather(values_local, "section", axis=1, tiled=True)
    key_count = key_block.shape[1]
    key_heads = key_block.reshape(count, key_count, local_heads, HD)
    value_heads = value_block.reshape(count, key_count, local_heads, HD)
    scores = jnp.einsum(
        "nqhd,nkhd->nhqk", queries, key_heads, preferred_element_type=jnp.float32
    ) * HD ** (-0.5)
    new_max = jnp.maximum(row_max, jnp.max(scores, axis=3))
    expo = jnp.exp(scores - new_max[..., None])
    totals = jnp.sum(expo, axis=3)
    running = jnp.einsum(
        "nhqk,nkhd->nhqd",
        expo.astype(jnp.bfloat16),
        value_heads,
        preferred_element_type=jnp.float32,
    )
    row_max, totals, running = (new_max, totals, running)
    mixed = (running / totals[..., None]).astype(jnp.bfloat16)
    mixed = mixed.transpose(0, 2, 1, 3).reshape(count, tok_local, head_cols)
    group_terms = jnp.einsum(
        "ntc,rnc->ntr",
        mixed,
        lax.all_gather(w_out, "section", axis=0, tiled=True),
        preferred_element_type=jnp.float32,
    )
    attended = lax.psum(group_terms.astype(jnp.bfloat16), "tp").astype(jnp.float32)
    return final_layer(hidden + attended, w_final)


def per_device(
    student_noise,
    renoise_noise,
    patch_slot,
    renoise_step,
    prompt_ids,
    text_table,
    student_in,
    student_qkv,
    student_out,
    student_final,
    real_in,
    real_qkv,
    real_out,
    real_final,
    fake_in,
    fake_qkv,
    fake_out,
    fake_final,
):
    vocab_local = text_table.shape[0]
    first_row = lax.axis_index(("section", "tp")) * vocab_local
    prompt_row = prompt_ids[0] - first_row
    matches = (prompt_row[:, None] == jnp.arange(vocab_local, dtype=jnp.int32)[None, :]).astype(
        jnp.bfloat16
    )
    counts = jnp.sum(matches.astype(jnp.float32), axis=0).astype(jnp.bfloat16)
    partial_pool = jnp.dot(counts, text_table, preferred_element_type=jnp.float32)
    pooled = lax.psum(partial_pool, ("section", "tp")) / prompt_ids.shape[1]
    condition = place_embed(patch_slot[0]) + pooled[None, :]
    start_noise = student_noise[0]
    velocity = networks(
        start_noise[None],
        jnp.ones((1,), jnp.float32),
        condition,
        student_in[None],
        student_qkv[:, None],
        student_out[:, None],
        student_final[None],
    )[0]
    clean = start_noise - velocity
    step_time = renoise_step[0].astype(jnp.float32) / 1000.0
    noisy = (1.0 - step_time) * clean + step_time * renoise_noise[0]
    step_row = jnp.full((1,), step_time, jnp.float32)
    real_velocity = networks(
        noisy[None],
        step_row,
        condition,
        real_in[None],
        real_qkv[:, None],
        real_out[:, None],
        real_final[None],
    )[0]
    fake_velocity = networks(
        noisy[None],
        step_row,
        condition,
        fake_in[None],
        fake_qkv[:, None],
        fake_out[:, None],
        fake_final[None],
    )[0]
    pred_real = noisy - step_time * real_velocity
    pred_fake = noisy - step_time * fake_velocity
    local_spread = jnp.sum(jnp.abs(clean - pred_real))
    entries = noisy.shape[0] * lax.axis_size("section") * noisy.shape[1]
    spread = lax.psum(local_spread, "section") / entries + 1e-05
    return ((pred_fake - pred_real) / spread)[None]


MESH = pl.DeviceIdType.MESH
NETS = 3


def dot(a, b):
    return jnp.dot(a, b, preferred_element_type=jnp.float32)


def step_kernel(
    pool_ref, pack_ref, noise_ref, table_ref, time_ref, when_ref, win_ref,
    wq0_ref, wq1_ref, wq2_ref, wo0_ref, wo1_ref, wo2_ref,
    out_ref,
    pool_sum, pool_sec, pool_tp, pack_all, noise_all, row_hot, col_hot, zin, cond, hid, normed,
    far_send, far_recv, cross_send, cross_recv, near_send, near_recv, own, qkv,
    mix, z_send, z_recv, z_own, f_mine, f_sib, f_pair, f_cross, flow_pack, grad_pack, clean, noisy,
    send_sem, recv_sem,
):
    wq = (wq0_ref, wq1_ref, wq2_ref)
    wo = (wo0_ref, wo1_ref, wo2_ref)
    sec = lax.axis_index("section")
    tp = lax.axis_index("tp")
    core = lax.rem(sec, 2)
    sib = sec + 1 - 2 * core
    cross = lax.rem(sec + 2, 4)
    diag = lax.rem(sib + 2, 4)
    tok = pack_ref.shape[0]
    total = 4 * tok
    feat = hid.shape[2]
    half = total // 2
    chunks = ((0, half), (half, half))
    tile = tok
    counter = [0]
    sends = []

    def send(src, dst, where):
        at = counter[0]
        counter[0] += 1
        copy = pltpu.make_async_remote_copy(
            src_ref=src, dst_ref=dst, send_sem=send_sem.at[at], recv_sem=recv_sem.at[at],
            device_id=where, device_id_type=MESH,
        )
        copy.start()
        sends.append(copy)
        return copy

    def at_sec(index):
        return {"section": index}

    def at_tp(index):
        return {"tp": index}

    tps = [lax.rem(tp + step, 4) for step in range(1, 4)]
    barrier = pltpu.get_barrier_semaphore()
    for where in [at_sec(sib), at_sec(cross), at_sec(diag)] + [at_tp(index) for index in tps]:
        pl.semaphore_signal(barrier, inc=1, device_id=where, device_id_type=MESH)
    pl.semaphore_wait(barrier, 6)

    others = (sib, cross, diag)
    got_pack = [send(pack_ref, pack_all.at[sec], at_sec(index)) for index in others]
    got_pool = [send(pool_ref, pool_sec.at[slot], at_sec(index)) for slot, index in enumerate(others)]
    pack_all[sec] = pack_ref[...]
    noise_all[sec] = noise_ref[...]
    for copy in got_pool:
        copy.wait_recv()
    pool_sum[...] = (pool_ref[...] + pool_sec[0]) + (pool_sec[1] + pool_sec[2])
    got_pool = [send(pool_sum, pool_tp.at[slot], at_tp(index)) for slot, index in enumerate(tps)]
    for copy in got_pack:
        copy.wait_recv()
    for block in range(4):
        rows = pl.ds(block * tok, tok)
        packed = pack_all[block]
        lane = lax.broadcasted_iota(jnp.int32, (tok, 128), 1)
        lane = jnp.where(lane >= 64, lane - 64, lane).astype(jnp.float32)
        wide = packed.astype(jnp.float32)
        row_hot[rows, :] = jnp.where(lane == wide[:, 64:65], 1.0, 0.0).astype(jnp.bfloat16)
        col_hot[rows, :] = jnp.where(lane == wide[:, 65:66], 1.0, 0.0).astype(jnp.bfloat16)
        zin[rows, :] = packed[:, :64]
    for copy in got_pool:
        copy.wait_recv()
    pooled = (pool_sum[...] + pool_tp[0]) + (pool_tp[1] + pool_tp[2])
    pool_sum_all = pool_sec.at[0]
    pool_sum_all[...] = pooled

    def tiles(start, size, body):
        @pl.loop(0, size // tile)
        def _(index):
            body(pl.ds(pl.multiple_of(start + index * tile, tile), tile))

    def place(rows):
        for part in range(4):
            hot = row_hot if part < 2 else col_hot
            cond[part, rows, :] = dot(hot[rows, :], table_ref[part % 2]) + pool_sum_all[part : part + 1, :]

    tiles(0, total, place)

    def embed(net):
        when = 0 if net == 0 else 1

        def body(rows):
            latent = zin[rows, :]
            squares = jnp.zeros((tile, 1), jnp.float32)
            for part in range(4):
                values = dot(latent, win_ref[net, part]) + cond[part, rows, :] + time_ref[when, part]
                squares += jnp.sum(values * values, axis=1, keepdims=True)
            values = dot(latent, win_ref[net, sec]) + cond[sec, rows, :] + time_ref[when, sec]
            hid[net, rows, :] = values
            scale = lax.rsqrt(squares / (4 * feat) + 1e-06)
            normed[net, rows, :] = (values * scale).astype(jnp.bfloat16)

        tiles(0, total, body)

    def part_of(net, rows, target):
        columns = pl.ds(pl.multiple_of(target * 128, 128), 128)
        left = normed[net, rows, :]
        return jnp.concatenate([dot(left, wq[net][kind, :, columns]) for kind in range(3)], axis=1)

    def project(net):
        far = []
        for start, size in chunks:
            def body(rows):
                far_send[net, rows, :] = part_of(net, rows, diag).astype(jnp.bfloat16)

            tiles(start, size, body)
            rows = pl.ds(start, size)
            far.append(send(far_send.at[net, rows], far_recv.at[net, rows], at_sec(sib)))
        crossed, near = [], []
        for index, (start, size) in enumerate(chunks):
            far[index].wait_recv()

            def body(rows):
                value = part_of(net, rows, cross)
                cross_send[net, rows, :] = (value + far_recv[net, rows, :].astype(jnp.float32)).astype(jnp.bfloat16)

            tiles(start, size, body)
            rows = pl.ds(start, size)
            crossed.append(send(cross_send.at[net, rows], cross_recv.at[net, rows], at_sec(cross)))
        for start, size in chunks:
            def body(rows):
                near_send[net, rows, :] = part_of(net, rows, sib).astype(jnp.bfloat16)

            tiles(start, size, body)
            rows = pl.ds(start, size)
            near.append(send(near_send.at[net, rows], near_recv.at[net, rows], at_sec(sib)))

        def body(rows):
            own[net, rows, :] = part_of(net, rows, sec)

        tiles(0, total, body)
        return crossed, near

    def attend(net, pending):
        crossed, near = pending
        for index, (start, size) in enumerate(chunks):
            near[index].wait_recv()
            crossed[index].wait_recv()

            def body(rows):
                value = own[net, rows, :] + near_recv[net, rows, :].astype(jnp.float32)
                value = value + cross_recv[net, rows, :].astype(jnp.float32)
                qkv[net, rows, :] = value.astype(jnp.bfloat16)

            tiles(start, size, body)
        direct = []
        for start, size in chunks:
            def body(rows):
                query = qkv[net, rows, 0:128]
                keys = qkv[net, :, 128:256]
                values = qkv[net, :, 256:384]
                low = lax.broadcasted_iota(jnp.int32, (tile, 128), 1) < HD
                results = []
                for head in range(2):
                    kept = jnp.where(low if head == 0 else jnp.logical_not(low), query.astype(jnp.float32), 0.0)
                    scores = lax.dot_general(
                        kept.astype(jnp.bfloat16), keys, (((1,), (1,)), ((), ())),
                        preferred_element_type=jnp.float32,
                    ) * HD ** (-0.5)
                    expo = jnp.exp(scores - jnp.max(scores, axis=1, keepdims=True))
                    sums = jnp.sum(expo, axis=1, keepdims=True)
                    results.append(dot(expo.astype(jnp.bfloat16), values) / sums)
                mix[net, sec, rows, :] = jnp.where(low, results[0], results[1]).astype(jnp.bfloat16)

            tiles(start, size, body)
            rows = pl.ds(start, size)
            piece = mix.at[net, sec, rows]
            direct.append((send(piece, piece, at_sec(cross)), send(piece, piece, at_sec(sib))))
        return direct

    def forward(net, direct):
        result = []
        for index, (start, size) in enumerate(chunks):
            direct[index][0].wait_recv()
            piece = mix.at[net, cross, pl.ds(start, size)]
            result.append(send(piece, piece, at_sec(sib)))
        return result

    def outward(net, direct, passed):
        for index in range(len(chunks)):
            direct[index][1].wait_recv()
            passed[index].wait_recv()

        def term(slot):
            rows = pl.ds(pl.multiple_of(slot * tok, tok), tok)
            left = jnp.concatenate([mix[net, index, rows, :] for index in range(4)], axis=1)
            return lax.dot_general(
                left, wo[net][...], (((1,), (1,)), ((), ())), preferred_element_type=jnp.float32
            ).astype(jnp.bfloat16)

        pending = []
        for step in (2, 1, 3):
            z_send[net, step - 1] = term(tps[step - 1])
            pending.append(send(z_send.at[net, step - 1], z_recv.at[net, step - 1], at_tp(tps[step - 1])))
        z_own[net] = term(tp)
        return pending

    def finish(net, pending):
        for copy in pending:
            copy.wait_recv()
        rows = pl.ds(pl.multiple_of(tp * tok, tok), tok)
        summed = z_own[net].astype(jnp.float32)
        for step in range(3):
            summed = summed + z_recv[net, step].astype(jnp.float32)
        after = hid[net, rows, :] + summed
        squares = jnp.sum(after * after, axis=1, keepdims=True)
        f_mine[net, :, 0:64] = lax.dot_general(
            after.astype(jnp.bfloat16), win_ref[NETS + net, sec], (((1,), (1,)), ((), ())),
            preferred_element_type=jnp.float32,
        )
        f_mine[net, :, 64:128] = jnp.broadcast_to(squares, (tok, 64))
        return send(f_mine.at[net], f_sib.at[net], at_sec(sib))

    def pair(net, copy):
        copy.wait_recv()
        f_pair[net] = f_mine[net] + f_sib[net]
        return send(f_pair.at[net], f_cross.at[net], at_sec(cross))

    def scaled(net, copy):
        copy.wait_recv()
        summed = f_pair[net] + f_cross[net]
        return summed[:, 0:64] * lax.rsqrt(summed[:, 64:128] / (4 * feat) + 1e-06)

    def pack_into(ref, value):
        ref[tp, 0 : tok // 2, 0:64] = value[: tok // 2]
        ref[tp, 0 : tok // 2, 64:128] = value[tok // 2 :]

    def to_groups(ref):
        return [send(ref.at[tp], ref.at[tp], at_tp(index)) for index in tps]

    embed(0)
    pending = project(0)
    direct = attend(0, pending)
    passed = forward(0, direct)
    got_noise = [send(noise_ref, noise_all.at[sec], at_sec(index)) for index in others]
    pending = outward(0, direct, passed)
    pack_into(flow_pack, scaled(0, pair(0, finish(0, pending))))
    pending = to_groups(flow_pack)
    for copy in got_noise:
        copy.wait_recv()
    for copy in pending:
        copy.wait_recv()
    moment = when_ref[0:1, 0:64]
    for block in range(4):
        both = noise_all[block]
        packed = flow_pack[block]
        for side in range(2):
            rows = pl.ds(block * tok + side * (tok // 2), tok // 2)
            local = slice(side * (tok // 2), (side + 1) * (tok // 2))
            start = both[local, 0:64] - packed[:, side * 64 : side * 64 + 64]
            clean[rows, :] = start
            mixed = (1.0 - moment) * start + moment * both[local, 64:128]
            noisy[rows, :] = mixed
            zin[rows, :] = mixed.astype(jnp.bfloat16)
    embed(1)
    pending = project(1)
    embed(2)
    direct = attend(1, pending)
    pending = project(2)
    passed = forward(1, direct)
    real_terms = outward(1, direct, passed)
    direct = attend(2, pending)
    passed = forward(2, direct)
    fake_terms = outward(2, direct, passed)
    real_pair = pair(1, finish(1, real_terms))
    real_flow = scaled(1, real_pair)
    rows = pl.ds(pl.multiple_of(tp * tok, tok), tok)
    real = noisy[rows, :] - moment * real_flow
    spread = jnp.sum(jnp.abs(clean[rows, :] - real), axis=1, keepdims=True)
    spread = jnp.sum(spread, axis=0, keepdims=True)
    grad_pack[tp, tok // 2 : tok // 2 + 8, :] = jnp.broadcast_to(spread, (8, 128))
    fake_flow = scaled(2, pair(2, finish(2, fake_terms)))
    fake = noisy[rows, :] - moment * fake_flow
    pack_into(grad_pack, fake - real)
    pending = to_groups(grad_pack)
    for copy in pending:
        copy.wait_recv()
    spread = jnp.zeros((1, 64), jnp.float32)
    for block in range(4):
        spread = spread + grad_pack[block, tok // 2 : tok // 2 + 1, 0:64]
    spread = spread / (total * 64) + 1e-05
    packed = grad_pack[sec]
    out_ref[0 : tok // 2, :] = packed[0 : tok // 2, 0:64] / spread
    out_ref[tok // 2 : tok, :] = packed[0 : tok // 2, 64:128] / spread
    for copy in sends:
        copy.wait_send()


def step_call(*operands):
    tok, feat, total = operands[1].shape[0], operands[0].shape[1], 4 * operands[1].shape[0]
    f32, bf16 = jnp.float32, jnp.bfloat16
    shapes = [
        ((8, feat), f32), ((3, 8, feat), f32), ((3, 8, feat), f32),
        ((4, tok, 128), bf16), ((4, tok, 128), f32),
        ((total, 128), bf16), ((total, 128), bf16), ((total, 64), bf16),
        ((4, total, feat), f32), ((NETS, total, feat), f32), ((NETS, total, feat), bf16),
    ]
    shapes += [((NETS, total, 384), bf16)] * 6
    shapes += [((NETS, total, 384), f32), ((NETS, total, 384), bf16)]
    shapes += [((NETS, 4, total, 128), bf16), ((NETS, 3, tok, feat), bf16), ((NETS, 3, tok, feat), bf16)]
    shapes += [((NETS, tok, feat), bf16)] + [((NETS, tok, 128), f32)] * 4
    shapes += [((4, tok // 2, 128), f32), ((4, tok // 2 + 8, 128), f32), ((total, 64), f32), ((total, 64), f32)]
    count = 3 * 4 + NETS * (6 + 6 + 3 + 2) + 6
    return pl.pallas_call(
        step_kernel,
        out_shape=jax.ShapeDtypeStruct((tok, 64), f32),
        in_specs=[pl.BlockSpec(memory_space=pltpu.VMEM)] * len(operands),
        out_specs=pl.BlockSpec(memory_space=pltpu.VMEM),
        scratch_shapes=[pltpu.VMEM(shape, kind) for shape, kind in shapes]
        + [pltpu.SemaphoreType.DMA((count,)), pltpu.SemaphoreType.DMA((count,))],
        compiler_params=pltpu.CompilerParams(
            collective_id=0, has_side_effects=True, vmem_limit_bytes=60 * 2**20
        ),
    )(*operands)


def by_features(
    student_noise, renoise_noise, patch_slot, renoise_step, prompt_ids, text_table,
    student_in, student_qkv, student_out, student_final,
    real_in, real_qkv, real_out, real_final,
    fake_in, fake_qkv, fake_out, fake_final,
):
    f32, bf16 = jnp.float32, jnp.bfloat16
    quarter = D // 4
    vocab_local = text_table.shape[0]
    first_row = lax.axis_index(("section", "tp")) * vocab_local
    prompt_row = prompt_ids[0] - first_row
    matches = (prompt_row[:, None] == jnp.arange(vocab_local, dtype=jnp.int32)[None, :]).astype(bf16)
    counts = jnp.sum(matches.astype(f32), axis=0).astype(bf16)
    pool = jnp.dot(counts, text_table, preferred_element_type=f32) / prompt_ids.shape[1]
    pool = jnp.pad(pool.reshape(4, quarter), ((0, 4), (0, 0)))
    slots = patch_slot[0]
    places = jnp.stack([slots // GRID_W, slots % GRID_W], axis=1).astype(bf16)
    pack = jnp.concatenate([student_noise[0].astype(bf16), jnp.pad(places, ((0, 0), (0, 62)))], axis=1)
    noise = jnp.concatenate([student_noise[0], renoise_noise[0]], axis=1)
    frequency = jnp.exp(-math.log(10000.0) * jnp.arange(quarter, dtype=f32) / quarter)
    angle = jnp.arange(64, dtype=f32)[:, None] * frequency[None, :]
    table = jnp.stack([jnp.sin(angle), jnp.cos(angle)])
    high = lax.reduce_precision(table, 8, 7)
    table = jnp.concatenate([high, table - high], axis=1).astype(bf16)
    moment = renoise_step[0].astype(f32) / 1000.0
    times = jnp.stack([time_embed(jnp.float32(1.0)), time_embed(moment)]).reshape(2, 4, 1, quarter)
    thin = jnp.stack([student_in, real_in, fake_in, student_final.T, real_final.T, fake_final.T])
    thin = thin.reshape(2 * NETS, 64, 4, quarter).transpose(0, 2, 1, 3)

    def by_kind(weight):
        return weight.transpose(1, 0, 2)

    result = step_call(
        pool, pack, noise, table, times, jnp.full((8, 128), moment, f32), thin,
        by_kind(student_qkv), by_kind(real_qkv), by_kind(fake_qkv),
        student_out, real_out, fake_out,
    )
    return result[None]


def solution(mesh):
    placed = (
        P("rep", "section", None),
        P("rep", "section", None),
        P("rep", "section"),
        P("rep"),
        P("rep", None),
        P(("section", "tp"), None),
        P(),
        P("section", None, "tp"),
        P("section", "tp"),
        P(),
        P(),
        P("section", None, "tp"),
        P("section", "tp"),
        P(),
        P(),
        P("section", None, "tp"),
        P("section", "tp"),
        P(),
    )
    sizes = dict(mesh.shape)
    small = sizes["section"] == 4 and sizes["tp"] == 4 and sizes["rep"] == 2
    return jax.shard_map(
        by_features if small else per_device, mesh=mesh, in_specs=placed, out_specs=P("rep", "section", None), check_vma=False
    )
```

```python
import math

import jax
import jax.numpy as jnp
from jax import lax
from jax.experimental import pallas as pl
from jax.experimental.pallas import tpu as pltpu
from jax.sharding import PartitionSpec as P

D = 2432
HD = 64
GRID_W = 64


def time_embed(step_time):
    half_width = D // 2
    frequency = jnp.exp(-math.log(10000.0) * jnp.arange(half_width, dtype=jnp.float32) / half_width)
    angles = 1000.0 * step_time * frequency
    return jnp.concatenate([jnp.cos(angles), jnp.sin(angles)])


def place_embed(slots):
    quarter = D // 4
    frequency = jnp.exp(-math.log(10000.0) * jnp.arange(quarter, dtype=jnp.float32) / quarter)
    row_angle = (slots // GRID_W).astype(jnp.float32)[:, None] * frequency[None, :]
    col_angle = (slots % GRID_W).astype(jnp.float32)[:, None] * frequency[None, :]
    return jnp.concatenate(
        [jnp.sin(row_angle), jnp.cos(row_angle), jnp.sin(col_angle), jnp.cos(col_angle)], axis=1
    )


def rms_norm(values):
    return values * lax.rsqrt(jnp.mean(values * values, axis=-1, keepdims=True) + 1e-06)


def final_layer(after, w_final):
    return jnp.einsum(
        "ntd,ndc->ntc",
        rms_norm(after).astype(jnp.bfloat16),
        w_final,
        preferred_element_type=jnp.float32,
    )


def networks(latents, step_times, condition, w_in, w_qkv, w_out, w_final):
    count = latents.shape[0]
    tok_local = latents.shape[1]
    head_cols = w_out.shape[2]
    local_heads = head_cols // HD
    hidden = jnp.einsum(
        "ntc,ncd->ntd", latents.astype(jnp.bfloat16), w_in, preferred_element_type=jnp.float32
    )
    hidden = hidden + condition[None, :, :] + jax.vmap(time_embed)(step_times)[:, None, :]
    normed = rms_norm(hidden).astype(jnp.bfloat16)
    projected = jnp.einsum(
        "ntd,dnkc->ntkc",
        normed,
        lax.all_gather(w_qkv, "section", axis=0, tiled=True),
        preferred_element_type=jnp.float32,
    )
    projected = projected.astype(jnp.bfloat16)
    queries = projected[:, :, 0].reshape(count, tok_local, local_heads, HD)
    keys_local = projected[:, :, 1]
    values_local = projected[:, :, 2]
    row_max = jnp.full((count, local_heads, tok_local), -1e30, jnp.float32)
    key_block = lax.all_gather(keys_local, "section", axis=1, tiled=True)
    value_block = lax.all_gather(values_local, "section", axis=1, tiled=True)
    key_count = key_block.shape[1]
    key_heads = key_block.reshape(count, key_count, local_heads, HD)
    value_heads = value_block.reshape(count, key_count, local_heads, HD)
    scores = jnp.einsum(
        "nqhd,nkhd->nhqk", queries, key_heads, preferred_element_type=jnp.float32
    ) * HD ** (-0.5)
    new_max = jnp.maximum(row_max, jnp.max(scores, axis=3))
    expo = jnp.exp(scores - new_max[..., None])
    totals = jnp.sum(expo, axis=3)
    running = jnp.einsum(
        "nhqk,nkhd->nhqd",
        expo.astype(jnp.bfloat16),
        value_heads,
        preferred_element_type=jnp.float32,
    )
    row_max, totals, running = (new_max, totals, running)
    mixed = (running / totals[..., None]).astype(jnp.bfloat16)
    mixed = mixed.transpose(0, 2, 1, 3).reshape(count, tok_local, head_cols)
    group_terms = jnp.einsum(
        "ntc,rnc->ntr",
        mixed,
        lax.all_gather(w_out, "section", axis=0, tiled=True),
        preferred_element_type=jnp.float32,
    )
    attended = lax.psum(group_terms.astype(jnp.bfloat16), "tp").astype(jnp.float32)
    return final_layer(hidden + attended, w_final)


def per_device(
    student_noise,
    renoise_noise,
    patch_slot,
    renoise_step,
    prompt_ids,
    text_table,
    student_in,
    student_qkv,
    student_out,
    student_final,
    real_in,
    real_qkv,
    real_out,
    real_final,
    fake_in,
    fake_qkv,
    fake_out,
    fake_final,
):
    vocab_local = text_table.shape[0]
    first_row = lax.axis_index(("section", "tp")) * vocab_local
    prompt_row = prompt_ids[0] - first_row
    matches = (prompt_row[:, None] == jnp.arange(vocab_local, dtype=jnp.int32)[None, :]).astype(
        jnp.bfloat16
    )
    counts = jnp.sum(matches.astype(jnp.float32), axis=0).astype(jnp.bfloat16)
    partial_pool = jnp.dot(counts, text_table, preferred_element_type=jnp.float32)
    pooled = lax.psum(partial_pool, ("section", "tp")) / prompt_ids.shape[1]
    condition = place_embed(patch_slot[0]) + pooled[None, :]
    start_noise = student_noise[0]
    velocity = networks(
        start_noise[None],
        jnp.ones((1,), jnp.float32),
        condition,
        student_in[None],
        student_qkv[:, None],
        student_out[:, None],
        student_final[None],
    )[0]
    clean = start_noise - velocity
    step_time = renoise_step[0].astype(jnp.float32) / 1000.0
    noisy = (1.0 - step_time) * clean + step_time * renoise_noise[0]
    step_row = jnp.full((1,), step_time, jnp.float32)
    real_velocity = networks(
        noisy[None],
        step_row,
        condition,
        real_in[None],
        real_qkv[:, None],
        real_out[:, None],
        real_final[None],
    )[0]
    fake_velocity = networks(
        noisy[None],
        step_row,
        condition,
        fake_in[None],
        fake_qkv[:, None],
        fake_out[:, None],
        fake_final[None],
    )[0]
    pred_real = noisy - step_time * real_velocity
    pred_fake = noisy - step_time * fake_velocity
    local_spread = jnp.sum(jnp.abs(clean - pred_real))
    entries = noisy.shape[0] * lax.axis_size("section") * noisy.shape[1]
    spread = lax.psum(local_spread, "section") / entries + 1e-05
    return ((pred_fake - pred_real) / spread)[None]


MESH = pl.DeviceIdType.MESH
NETS = 3


def dot(a, b):
    return jnp.dot(a, b, preferred_element_type=jnp.float32)


def step_kernel(
    pool_ref, pack_ref, noise_ref, table_ref, time_ref, when_ref, win_ref,
    wq0_ref, wq1_ref, wq2_ref, wo0_ref, wo1_ref, wo2_ref,
    out_ref,
    pool_sum, pool_sec, pool_tp, pack_all, noise_all, row_hot, col_hot, zin, cond, hid, normed,
    far_send, far_recv, cross_send, cross_recv, near_send, near_recv, own, qkv,
    mix, z_send, z_recv, z_own, f_mine, f_sib, f_pair, f_cross, flow_pack, grad_pack, clean, noisy, shift, val_ones, wq_all, wo_all,
    send_sem, recv_sem, stage_sem,
):
    staged, staged_out = [], []
    for net, (source, source_out) in enumerate(((wq0_ref, wo0_ref), (wq1_ref, wo1_ref), (wq2_ref, wo2_ref))):
        staged.append(pltpu.make_async_copy(source, wq_all.at[net], stage_sem.at[2 * net]))
        staged_out.append(pltpu.make_async_copy(source_out, wo_all.at[net], stage_sem.at[2 * net + 1]))
    for copy in staged + staged_out:
        copy.start()
    sec = lax.axis_index("section")
    tp = lax.axis_index("tp")
    core = lax.rem(sec, 2)
    sib = sec + 1 - 2 * core
    cross = lax.rem(sec + 2, 4)
    diag = lax.rem(sib + 2, 4)
    tok = pack_ref.shape[0]
    total = 4 * tok
    feat = hid.shape[2]
    half = total // 2
    chunks = ((0, half), (half, half))
    tile = tok
    counter = [0]
    sends = []

    def send(src, dst, where):
        at = counter[0]
        counter[0] += 1
        copy = pltpu.make_async_remote_copy(
            src_ref=src, dst_ref=dst, send_sem=send_sem.at[at], recv_sem=recv_sem.at[at],
            device_id=where, device_id_type=MESH,
        )
        copy.start()
        sends.append(copy)
        return copy

    def at_sec(index):
        return {"section": index}

    def at_tp(index):
        return {"tp": index}

    tps = [lax.rem(tp + step, 4) for step in range(1, 4)]
    barrier = pltpu.get_barrier_semaphore()
    for where in [at_sec(sib), at_sec(cross), at_sec(diag)] + [at_tp(index) for index in tps]:
        pl.semaphore_signal(barrier, inc=1, device_id=where, device_id_type=MESH)
    pl.semaphore_wait(barrier, 6)

    others = (sib, cross, diag)
    got_pack = [send(pack_ref, pack_all.at[sec], at_sec(index)) for index in others]
    got_pool = [send(pool_ref, pool_sec.at[slot], at_sec(index)) for slot, index in enumerate(others)]
    pack_all[sec] = pack_ref[...]
    noise_all[sec] = noise_ref[...]
    for copy in got_pool:
        copy.wait_recv()
    pool_sum[...] = (pool_ref[...] + pool_sec[0]) + (pool_sec[1] + pool_sec[2])
    got_pool = [send(pool_sum, pool_tp.at[slot], at_tp(index)) for slot, index in enumerate(tps)]
    for copy in got_pack:
        copy.wait_recv()
    for block in range(4):
        rows = pl.ds(block * tok, tok)
        packed = pack_all[block]
        lane = lax.broadcasted_iota(jnp.int32, (tok, 128), 1)
        lane = jnp.where(lane >= 64, lane - 64, lane).astype(jnp.float32)
        wide = packed.astype(jnp.float32)
        row_hot[rows, :] = jnp.where(lane == wide[:, 64:65], 1.0, 0.0).astype(jnp.bfloat16)
        col_hot[rows, :] = jnp.where(lane == wide[:, 65:66], 1.0, 0.0).astype(jnp.bfloat16)
        zin[rows, :] = packed[:, :64]
    def tiles(start, size, body):
        @pl.loop(0, size // tile)
        def _(index):
            body(pl.ds(pl.multiple_of(start + index * tile, tile), tile))

    def place(rows):
        for part in range(4):
            hot = row_hot if part < 2 else col_hot
            cond[part, rows, :] = dot(hot[rows, :], table_ref[part % 2])

    tiles(0, total, place)
    for copy in got_pool:
        copy.wait_recv()
    pooled = (pool_sum[...] + pool_tp[0]) + (pool_tp[1] + pool_tp[2])
    for part in range(4):
        for when in range(2):
            shift[when, part] = pooled[part : part + 1, :] + time_ref[when, part]

    def embed(net):
        when = 0 if net == 0 else 1

        def body(rows):
            latent = zin[rows, :]
            squares = jnp.zeros((tile, 1), jnp.float32)
            for part in range(4):
                values = dot(latent, win_ref[net, part]) + cond[part, rows, :] + shift[when, part]
                squares += jnp.sum(values * values, axis=1, keepdims=True)
            values = dot(latent, win_ref[net, sec]) + cond[sec, rows, :] + shift[when, sec]
            hid[net, rows, :] = values
            scale = lax.rsqrt(squares / (4 * feat) + 1e-06)
            normed[net, rows, :] = (values * scale).astype(jnp.bfloat16)

        tiles(0, total, body)

    def part_of(net, rows, target):
        columns = pl.ds(pl.multiple_of(target * 128, 128), 128)
        right = jnp.concatenate([wq_all[net, kind, :, columns] for kind in range(3)], axis=1)
        return dot(normed[net, rows, :], right)

    def project(net):
        staged[net].wait()
        far = []
        for start, size in chunks:
            def body(rows):
                far_send[net, rows, :] = part_of(net, rows, diag).astype(jnp.bfloat16)

            body(pl.ds(start, size))
            rows = pl.ds(start, size)
            far.append(send(far_send.at[net, rows], far_recv.at[net, rows], at_sec(sib)))
        crossed, near = [], []
        for index, (start, size) in enumerate(chunks):
            far[index].wait_recv()

            def body(rows):
                value = part_of(net, rows, cross)
                cross_send[net, rows, :] = (value + far_recv[net, rows, :].astype(jnp.float32)).astype(jnp.bfloat16)

            body(pl.ds(start, size))
            rows = pl.ds(start, size)
            crossed.append(send(cross_send.at[net, rows], cross_recv.at[net, rows], at_sec(cross)))
        for start, size in chunks:
            def body(rows):
                near_send[net, rows, :] = part_of(net, rows, sib).astype(jnp.bfloat16)

            body(pl.ds(start, size))
            rows = pl.ds(start, size)
            near.append(send(near_send.at[net, rows], near_recv.at[net, rows], at_sec(sib)))

        def body(rows):
            own[net, rows, :] = part_of(net, rows, sec)

        for start, size in chunks:
            body(pl.ds(start, size))
        return crossed, near

    def attend(net, pending):
        crossed, near = pending
        for index, (start, size) in enumerate(chunks):
            near[index].wait_recv()
            crossed[index].wait_recv()

            def body(rows):
                value = own[net, rows, :] + near_recv[net, rows, :].astype(jnp.float32)
                value = value + cross_recv[net, rows, :].astype(jnp.float32)
                qkv[net, rows, :] = value.astype(jnp.bfloat16)
                left = lax.broadcasted_iota(jnp.int32, (tile, 128), 1) < HD
                val_ones[net, 0, rows, :] = jnp.where(left, value[:, 256:384], 1.0).astype(jnp.bfloat16)
                val_ones[net, 1, rows, :] = jnp.where(left, 1.0, value[:, 256:384]).astype(jnp.bfloat16)

            tiles(start, size, body)
        direct = []
        for start, size in chunks:
            def body(rows):
                query = qkv[net, rows, 0:128].astype(jnp.float32) * HD ** (-0.5)
                keys = qkv[net, :, 128:256]
                low = lax.broadcasted_iota(jnp.int32, (tile, 128), 1) < HD
                results = []
                for head in range(2):
                    kept = jnp.where(low if head == 0 else jnp.logical_not(low), query, 0.0)
                    scores = lax.dot_general(
                        kept.astype(jnp.bfloat16), keys, (((1,), (1,)), ((), ())),
                        preferred_element_type=jnp.float32,
                    )
                    expo = jnp.exp(scores - jnp.max(scores, axis=1, keepdims=True))
                    results.append(dot(expo.astype(jnp.bfloat16), val_ones[net, head]))
                sums = pltpu.roll(jnp.where(low, results[1], results[0]), HD, 1)
                mix[net, sec, rows, :] = (jnp.where(low, results[0], results[1]) / sums).astype(jnp.bfloat16)

            tiles(start, size, body)
            rows = pl.ds(start, size)
            piece = mix.at[net, sec, rows]
            direct.append((send(piece, piece, at_sec(cross)), send(piece, piece, at_sec(sib))))
        return direct

    def forward(net, direct):
        result = []
        for index, (start, size) in enumerate(chunks):
            direct[index][0].wait_recv()
            piece = mix.at[net, cross, pl.ds(start, size)]
            result.append(send(piece, piece, at_sec(sib)))
        return result

    def outward(net, direct, passed):
        for index in range(len(chunks)):
            direct[index][1].wait_recv()
            passed[index].wait_recv()

        def term(slot):
            rows = pl.ds(pl.multiple_of(slot * tok, tok), tok)
            left = jnp.concatenate([mix[net, index, rows, :] for index in range(4)], axis=1)
            return lax.dot_general(
                left, wo_all[net], (((1,), (1,)), ((), ())), preferred_element_type=jnp.float32
            ).astype(jnp.bfloat16)

        staged_out[net].wait()
        pending = []
        for step in (2, 1, 3):
            z_send[net, step - 1] = term(tps[step - 1])
            pending.append(send(z_send.at[net, step - 1], z_recv.at[net, step - 1], at_tp(tps[step - 1])))
        z_own[net] = term(tp)
        return pending

    def finish(net, pending):
        for copy in pending:
            copy.wait_recv()
        rows = pl.ds(pl.multiple_of(tp * tok, tok), tok)
        summed = z_own[net].astype(jnp.float32)
        for step in range(3):
            summed = summed + z_recv[net, step].astype(jnp.float32)
        after = hid[net, rows, :] + summed
        squares = jnp.sum(after * after, axis=1, keepdims=True)
        f_mine[net, :, 0:64] = lax.dot_general(
            after.astype(jnp.bfloat16), win_ref[NETS + net, sec], (((1,), (1,)), ((), ())),
            preferred_element_type=jnp.float32,
        )
        f_mine[net, :, 64:128] = jnp.broadcast_to(squares, (tok, 64))
        return send(f_mine.at[net], f_sib.at[net], at_sec(sib))

    def pair(net, copy):
        copy.wait_recv()
        f_pair[net] = f_mine[net] + f_sib[net]
        return send(f_pair.at[net], f_cross.at[net], at_sec(cross))

    def scaled(net, copy):
        copy.wait_recv()
        summed = f_pair[net] + f_cross[net]
        return summed[:, 0:64] * lax.rsqrt(summed[:, 64:128] / (4 * feat) + 1e-06)

    def pack_into(ref, value):
        ref[tp, 0 : tok // 2, 0:64] = value[: tok // 2]
        ref[tp, 0 : tok // 2, 64:128] = value[tok // 2 :]

    def to_groups(ref):
        return [send(ref.at[tp], ref.at[tp], at_tp(index)) for index in tps]

    embed(0)
    pending = project(0)
    direct = attend(0, pending)
    passed = forward(0, direct)
    got_noise = [send(noise_ref, noise_all.at[sec], at_sec(index)) for index in others]
    pending = outward(0, direct, passed)
    pack_into(flow_pack, scaled(0, pair(0, finish(0, pending))))
    pending = to_groups(flow_pack)
    for copy in got_noise:
        copy.wait_recv()
    for copy in pending:
        copy.wait_recv()
    moment = when_ref[0:1, 0:64]
    for block in range(4):
        both = noise_all[block]
        packed = flow_pack[block]
        for side in range(2):
            rows = pl.ds(block * tok + side * (tok // 2), tok // 2)
            local = slice(side * (tok // 2), (side + 1) * (tok // 2))
            start = both[local, 0:64] - packed[:, side * 64 : side * 64 + 64]
            clean[rows, :] = start
            mixed = (1.0 - moment) * start + moment * both[local, 64:128]
            noisy[rows, :] = mixed
            zin[rows, :] = mixed.astype(jnp.bfloat16)
    embed(1)
    pending = project(1)
    embed(2)
    direct = attend(1, pending)
    pending = project(2)
    passed = forward(1, direct)
    real_terms = outward(1, direct, passed)
    direct = attend(2, pending)
    passed = forward(2, direct)
    fake_terms = outward(2, direct, passed)
    real_pair = pair(1, finish(1, real_terms))
    real_flow = scaled(1, real_pair)
    rows = pl.ds(pl.multiple_of(tp * tok, tok), tok)
    real = noisy[rows, :] - moment * real_flow
    spread = jnp.sum(jnp.abs(clean[rows, :] - real), axis=1, keepdims=True)
    spread = jnp.sum(spread, axis=0, keepdims=True)
    grad_pack[tp, tok // 2 : tok // 2 + 8, :] = jnp.broadcast_to(spread, (8, 128))
    fake_flow = scaled(2, pair(2, finish(2, fake_terms)))
    fake = noisy[rows, :] - moment * fake_flow
    pack_into(grad_pack, fake - real)
    pending = to_groups(grad_pack)
    for copy in pending:
        copy.wait_recv()
    spread = jnp.zeros((1, 64), jnp.float32)
    for block in range(4):
        spread = spread + grad_pack[block, tok // 2 : tok // 2 + 1, 0:64]
    spread = spread / (total * 64) + 1e-05
    packed = grad_pack[sec]
    out_ref[0 : tok // 2, :] = packed[0 : tok // 2, 0:64] / spread
    out_ref[tok // 2 : tok, :] = packed[0 : tok // 2, 64:128] / spread
    for copy in sends:
        copy.wait_send()


def step_call(*operands):
    tok, feat, total = operands[1].shape[0], operands[0].shape[1], 4 * operands[1].shape[0]
    f32, bf16 = jnp.float32, jnp.bfloat16
    shapes = [
        ((8, feat), f32), ((3, 8, feat), f32), ((3, 8, feat), f32),
        ((4, tok, 128), bf16), ((4, tok, 128), f32),
        ((total, 128), bf16), ((total, 128), bf16), ((total, 64), bf16),
        ((4, total, feat), f32), ((NETS, total, feat), f32), ((NETS, total, feat), bf16),
    ]
    shapes += [((NETS, total, 384), bf16)] * 6
    shapes += [((NETS, total, 384), f32), ((NETS, total, 384), bf16)]
    shapes += [((NETS, 4, total, 128), bf16), ((NETS, 3, tok, feat), bf16), ((NETS, 3, tok, feat), bf16)]
    shapes += [((NETS, tok, feat), bf16)] + [((NETS, tok, 128), f32)] * 4
    shapes += [((4, tok // 2, 128), f32), ((4, tok // 2 + 8, 128), f32), ((total, 64), f32), ((total, 64), f32)]
    shapes += [((2, 4, 1, feat), f32), ((NETS, 2, total, 128), bf16)]
    shapes += [((NETS, 3, feat, 512), bf16), ((NETS, feat, 512), bf16)]
    count = 3 * 4 + NETS * (6 + 6 + 3 + 2) + 6
    return pl.pallas_call(
        step_kernel,
        out_shape=jax.ShapeDtypeStruct((tok, 64), f32),
        in_specs=[pl.BlockSpec(memory_space=pltpu.VMEM)] * (len(operands) - 6)
        + [pl.BlockSpec(memory_space=pl.ANY)] * 6,
        out_specs=pl.BlockSpec(memory_space=pltpu.VMEM),
        scratch_shapes=[pltpu.VMEM(shape, kind) for shape, kind in shapes]
        + [pltpu.SemaphoreType.DMA((count,)), pltpu.SemaphoreType.DMA((count,)), pltpu.SemaphoreType.DMA((6,))],
        compiler_params=pltpu.CompilerParams(
            collective_id=0, has_side_effects=True, vmem_limit_bytes=60 * 2**20
        ),
    )(*operands)


def by_features(
    student_noise, renoise_noise, patch_slot, renoise_step, prompt_ids, text_table,
    student_in, student_qkv, student_out, student_final,
    real_in, real_qkv, real_out, real_final,
    fake_in, fake_qkv, fake_out, fake_final,
):
    f32, bf16 = jnp.float32, jnp.bfloat16
    quarter = D // 4
    vocab_local = text_table.shape[0]
    first_row = lax.axis_index(("section", "tp")) * vocab_local
    prompt_row = prompt_ids[0] - first_row
    matches = (prompt_row[:, None] == jnp.arange(vocab_local, dtype=jnp.int32)[None, :]).astype(bf16)
    counts = jnp.sum(matches.astype(f32), axis=0).astype(bf16)
    pool = jnp.dot(counts, text_table, preferred_element_type=f32) / prompt_ids.shape[1]
    pool = jnp.pad(pool.reshape(4, quarter), ((0, 4), (0, 0)))
    slots = patch_slot[0]
    places = jnp.stack([slots // GRID_W, slots % GRID_W], axis=1).astype(bf16)
    pack = jnp.concatenate([student_noise[0].astype(bf16), jnp.pad(places, ((0, 0), (0, 62)))], axis=1)
    noise = jnp.concatenate([student_noise[0], renoise_noise[0]], axis=1)
    frequency = jnp.exp(-math.log(10000.0) * jnp.arange(quarter, dtype=f32) / quarter)
    angle = jnp.arange(64, dtype=f32)[:, None] * frequency[None, :]
    table = jnp.stack([jnp.sin(angle), jnp.cos(angle)])
    high = lax.reduce_precision(table, 8, 7)
    table = jnp.concatenate([high, table - high], axis=1).astype(bf16)
    moment = renoise_step[0].astype(f32) / 1000.0
    times = jnp.stack([time_embed(jnp.float32(1.0)), time_embed(moment)]).reshape(2, 4, 1, quarter)
    thin = jnp.stack([student_in, real_in, fake_in, student_final.T, real_final.T, fake_final.T])
    thin = thin.reshape(2 * NETS, 64, 4, quarter).transpose(0, 2, 1, 3)

    def by_kind(weight):
        return weight.transpose(1, 0, 2)

    result = step_call(
        pool, pack, noise, table, times, jnp.full((8, 128), moment, f32), thin,
        by_kind(student_qkv), by_kind(real_qkv), by_kind(fake_qkv),
        student_out, real_out, fake_out,
    )
    return result[None]


def solution(mesh):
    placed = (
        P("rep", "section", None),
        P("rep", "section", None),
        P("rep", "section"),
        P("rep"),
        P("rep", None),
        P(("section", "tp"), None),
        P(),
        P("section", None, "tp"),
        P("section", "tp"),
        P(),
        P(),
        P("section", None, "tp"),
        P("section", "tp"),
        P(),
        P(),
        P("section", None, "tp"),
        P("section", "tp"),
        P(),
    )
    sizes = dict(mesh.shape)
    small = sizes["section"] == 4 and sizes["tp"] == 4 and sizes["rep"] == 2
    return jax.shard_map(
        by_features if small else per_device, mesh=mesh, in_specs=placed, out_specs=P("rep", "section", None), check_vma=False
    )
```
